32 devices in a mesh: region: 2 (over x), member: 16 (over z, y, core).
Axes of the slice: x: 2, y: 2, z: 4, core: 2. Of those that a mesh axis runs over, the one named last changes fastest.
Arguments:
- analyses: bfloat16 [16, 1024, 1024], P('member', 'region'), may hold values from -6 to 6
- owners: int32 [4], replicated, may hold values from 0 to 15, as said below
- noise: bfloat16 [16, 1024, 1024], P('member', 'region'), may hold values from -24 to 24
- targets: bfloat16 [1024, 1024], P(('region', 'member')), may hold values from -6 to 6
- area_weight: float32 [1024], P(('region', 'member')), may hold values from 0.025 to 1.5
- enc_weight: bfloat16 [1024, 1024], replicated, may hold values from -0.1875 to 0.1875
- sample_inlet_matrix: bfloat16 [1024, 2048], replicated, may hold values from -0.1875 to 0.1875
- sample_outlet_matrix: bfloat16 [2048, 1024], replicated, may hold values from -0.125 to 0.125
Outputs:
- member_grad: bfloat16 [16, 1024, 1024], P('member', 'region')
- energy: float32 [1024], P(('region', 'member'))
The draws below stay inside these ranges and needn't reach their ends.
Inputs may be any that keep to these rules, and one draw needn't show every extreme that they name: `owners`: 4 distinct member indices, entry b naming the control member of block b; member 0 and member 16 - 1 are always among them.
All inputs are finite; a program needn't handle non-finite values.
Results may differ from the reference program's by a relative error of at most 0.005.
Values may be sent and summed in bfloat16 or wider, within the bound.
No kernel may reach another device: no remote copies, remote signals or barrier semaphores. Data moves between devices by JAX's collectives and lax.ppermute only.
A program may use at most 64 MiB of HBM per device.

```python
import math
import jax
import jax.numpy as jnp
from jax import lax

D = 1024
FFN = 2048
TOK_REG = 512
BLOCKS = 4
MEMBERS = 16
TOKENS = 1024
N_REGION = 2


def draw_owners(key, part):
    key = jax.random.fold_in(key, 11)
    key_pick, key_order = jax.random.split(key, 2)
    middle = jax.random.permutation(key_pick, MEMBERS - 2)[:BLOCKS - 2].astype(jnp.int32) + 1
    ends = jnp.array([0, MEMBERS - 1], jnp.int32)
    chosen = jnp.concatenate([ends, middle], axis=0)
    order = jax.random.permutation(key_order, BLOCKS)
    return chosen[order].astype(jnp.int32)


def draw_noise(key, part):
    key_base = jax.random.fold_in(key, 0)
    values = jax.random.normal(key_base, (MEMBERS, TOKENS, D), jnp.float32)
    return jnp.clip(values, -24.0, 24.0).astype(jnp.bfloat16)


def draw_area_weight(key, part):
    position = jnp.arange(TOKENS, dtype=jnp.float32) / TOKENS
    profile = jnp.exp(math.log(0.3) * (1.0 - position))
    jitter = jax.random.uniform(key, (TOKENS,), jnp.float32, 0.5, 1.5)
    return jnp.clip(profile * jitter, 0.025, 1.5)


def shard_levels(rng, extent, cuts, smallest, top_value):
    factor_of, own = 1.0, jax.random.fold_in(rng, 6)
    for dim, shards_of in cuts:
        draws = jnp.exp(jax.random.uniform(jax.random.fold_in(own, dim), (shards_of,), jnp.float32, smallest / len(cuts), top_value / len(cuts)))
        factor_of = factor_of * jnp.repeat(draws, extent[dim] // shards_of).reshape([-1 if axis == dim else 1 for axis in range(len(extent))])
    return factor_of


def bell_draw(stream_key, shape, scale, reach, cuts=(), kind=jnp.bfloat16):
    result = scale * jax.random.normal(stream_key, shape, jnp.float32)
    if cuts:
        result = result * shard_levels(stream_key, shape, cuts, -0.22, 0.18)
    return jnp.clip(result, -reach, reach).astype(kind)


def setup_inputs(seed: int = 0) -> dict:
    splits = jax.random.split(jax.random.key(seed), 9)
    analyses = bell_draw(splits[0], (MEMBERS, TOKENS, D), 1.0, 6.0, ((0, 16), (1, 2)))
    owners = draw_owners(jax.random.fold_in(splits[8], 71), 0)
    noise = draw_noise(jax.random.fold_in(splits[8], 71), 0)
    targets = bell_draw(splits[3], (TOKENS, D), 1.0, 6.0, ((0, 32),))
    area_weight = draw_area_weight(jax.random.fold_in(splits[8], 71), 0)
    enc_weight = bell_draw(splits[5], (D, D), D ** -0.5, 0.1875)
    sample_inlet_matrix = bell_draw(splits[6], (D, FFN), D ** -0.5, 0.1875)
    sample_outlet_matrix = bell_draw(splits[7], (FFN, D), FFN ** -0.5, 0.125)
    return dict(analyses=analyses, owners=owners, noise=noise, targets=targets, area_weight=area_weight, enc_weight=enc_weight, sample_inlet_matrix=sample_inlet_matrix, sample_outlet_matrix=sample_outlet_matrix)


epsilon = 1e-06

def apply_model(sample_hidden_vectors, sample_inlet_matrix, sample_outlet_matrix):
    features = sample_hidden_vectors.shape[-1]
    flat = sample_hidden_vectors.reshape(-1, features)
    normed = (flat * lax.rsqrt(lax.optimization_barrier(jnp.mean(flat * flat, axis=-1, keepdims=True)) + epsilon)).astype(jnp.bfloat16)
    hidden = jax.nn.gelu(jnp.dot(normed, sample_inlet_matrix, preferred_element_type=jnp.float32)).astype(jnp.bfloat16)
    output = flat + jnp.dot(hidden, sample_outlet_matrix, preferred_element_type=jnp.float32)
    return output.reshape(sample_hidden_vectors.shape).astype(jnp.bfloat16)

def spread_skill_loss(member_ensemble, goal_slice, coefficient_slice, coefficient_mean):
    members = member_ensemble.shape[0]
    features = member_ensemble.shape[2]
    values = member_ensemble.astype(jnp.float32)
    from_target = values - goal_slice.astype(jnp.float32)[None]
    spread = jnp.sqrt(lax.optimization_barrier(jnp.mean(from_target * from_target, axis=-1)) + epsilon)
    inner = jnp.einsum('mtd,jtd->tmj', values, values, precision=lax.Precision.HIGHEST)
    squares = jnp.diagonal(inner, axis1=1, axis2=2)
    pair_dist = jnp.sqrt((squares[:, :, None] + squares[:, None, :] - 2.0 * inner) / features + epsilon)
    positions = jnp.arange(members)
    diagonal_mask = positions[:, None] == positions[None, :]
    pair_coeff = jnp.where(diagonal_mask[None], 0.0, 1.0 / pair_dist).astype(jnp.bfloat16)
    coeff_float = pair_coeff.astype(jnp.float32)
    coeff_sum = lax.optimization_barrier(jnp.sum(coeff_float, axis=-1))
    combined = jnp.einsum('tmj,jtd->mtd', coeff_float, values, precision=lax.Precision.HIGHEST)
    weight_scale = coefficient_slice / coefficient_mean
    gradient = weight_scale[None, :, None] * (from_target / spread[:, :, None] - (jnp.transpose(coeff_sum)[:, :, None] * values - combined) / members)
    energy = weight_scale * (lax.optimization_barrier(jnp.mean(spread, axis=0)) - lax.optimization_barrier(jnp.sum(pair_dist, axis=(1, 2))) / (2.0 * members * members))
    return (gradient.astype(jnp.bfloat16), energy)

def reference(analyses, owners, noise, targets, area_weight, enc_weight, sample_inlet_matrix, sample_outlet_matrix):
    block_rows = TOK_REG // BLOCKS
    grouped = analyses.reshape(MEMBERS, N_REGION, BLOCKS, block_rows, D)
    pieces = []
    for block_index in range(BLOCKS):
        pieces.append(lax.dynamic_index_in_dim(grouped[:, :, block_index], owners[block_index].astype(jnp.int32), 0, keepdims=False))
    control = jnp.stack(pieces, axis=1).reshape(TOKENS, D)
    latent = jnp.dot(control, enc_weight, preferred_element_type=jnp.float32).astype(jnp.bfloat16)
    coefficient_mean = jnp.mean(area_weight)
    by_region = (latent.reshape(N_REGION, TOK_REG, D), jnp.transpose(noise.reshape(MEMBERS, N_REGION, TOK_REG, D), (1, 0, 2, 3)), targets.reshape(N_REGION, TOK_REG, D), area_weight.reshape(N_REGION, TOK_REG))

    def one_region(inputs):
        latent_part, noise_part, goal_slice, coefficient_slice = inputs
        sample_hidden_vectors = latent_part.astype(jnp.float32)[None] + noise_part.astype(jnp.float32)
        zone_prediction = apply_model(sample_hidden_vectors, sample_inlet_matrix, sample_outlet_matrix)
        return spread_skill_loss(zone_prediction, goal_slice, coefficient_slice, coefficient_mean)
    gradient, energy = lax.map(one_region, by_region)
    member_grad = jnp.transpose(gradient, (1, 0, 2, 3)).reshape(MEMBERS, TOKENS, D)
    return (member_grad, energy.reshape(TOKENS))
```

```python
import functools
import math

import jax
import jax.numpy as jnp
from jax import lax
from jax.experimental import pallas as pl
from jax.experimental.pallas import tpu as pltpu
from jax.sharding import PartitionSpec as P

EPSILON = 1e-06
TOKENS_AT_ONCE = 16
HIDDEN_PIECES = 4
BF16 = jnp.bfloat16
F32 = jnp.float32


def swap(value, axis, bit):
    size = lax.axis_size(axis)
    return lax.ppermute(value, axis, [(i, i ^ bit) for i in range(size)])


def bits_of(size):
    return [1 << i for i in range(size.bit_length() - 1)]


def control_rows(analyses, owners):
    members = lax.axis_size("member")
    me = lax.axis_index("member")
    _, rows, features = analyses.shape
    blocks = owners.shape[0]
    lanes = members // blocks
    own = rows // members
    my_lane, my_block = me % lanes, me // lanes
    block_here = jnp.sum(jnp.where(owners == me, jnp.arange(blocks, dtype=jnp.int32), 0))
    held = lax.dynamic_slice_in_dim(analyses[0], block_here * (rows // blocks), rows // blocks, 0)
    held = held.reshape(1, lanes, own, features)
    for bit in reversed(bits_of(lanes)):
        halves = held.reshape(held.shape[0], 2, held.shape[1] // 2, own, features)
        mine = (my_lane // bit) % 2
        keep = lax.dynamic_index_in_dim(halves, mine, 1, keepdims=False)
        give = lax.dynamic_index_in_dim(halves, 1 - mine, 1, keepdims=False)
        held = jnp.concatenate([keep, swap(give, "member", bit)], axis=0)
    held = held.reshape(lanes, own, features)
    picked = []
    for block in range(blocks):
        apart = (owners[block] % lanes) ^ my_lane
        place = jnp.int32(0)
        for step, bit in enumerate(reversed(bits_of(lanes))):
            place = place + ((apart // bit) % 2) * (1 << step)
        picked.append(lax.dynamic_index_in_dim(held, place, 0, keepdims=False))
    held = jnp.stack(picked, axis=0)
    owner_block = owners // lanes
    for bit in bits_of(blocks):
        halves = held.reshape(held.shape[0] // 2, 2, own, features)
        mine = (my_block // bit) % 2
        keep = lax.dynamic_index_in_dim(halves, mine, 1, keepdims=False)
        give = lax.dynamic_index_in_dim(halves, 1 - mine, 1, keepdims=False)
        got = swap(give, "member", bit * lanes)
        ids = jnp.arange(halves.shape[0], dtype=jnp.int32) * (2 * bit) + my_block % (2 * bit)
        from_there = ((owner_block[ids] ^ my_block) // bit) % 2 == 1
        held = jnp.where(from_there[:, None, None], got, keep)
    return held[0]


def total_weight(area_weight):
    total = jnp.full((8, 128), jnp.sum(area_weight), F32)
    for bit in bits_of(lax.axis_size("member")):
        total = total + swap(total, "member", bit)
    for bit in bits_of(lax.axis_size("region")):
        total = total + swap(total, "region", bit)
    return total


def network(noise, latent, hidden_piece, pieces):
    members, tokens, features = noise.shape
    states = (noise.astype(F32) + latent.astype(F32)[None]).reshape(members * tokens, features)
    mean = jnp.sum(states * states, axis=-1, keepdims=True) * (1.0 / features)
    normed = (states * lax.rsqrt(mean + EPSILON)).astype(BF16)
    total = states
    for piece in range(pieces):
        total = total + hidden_piece(normed, piece)
    return total.astype(BF16)


def score(forecast, targets, scale, members, tokens):
    rows, features = forecast.shape
    gram = lax.dot_general(
        forecast, forecast, (((1,), (1,)), ((), ())), preferred_element_type=F32
    )
    first = lax.broadcasted_iota(jnp.int32, (rows, rows), 0)
    second = lax.broadcasted_iota(jnp.int32, (rows, rows), 1)
    same_row = first == second
    same_token = (first % tokens) == (second % tokens)
    on_diagonal = jnp.where(same_row, gram, 0.0)
    down = jnp.sum(on_diagonal, axis=1, keepdims=True)
    across = jnp.sum(on_diagonal, axis=0, keepdims=True)
    squared = jnp.maximum((down + across - 2.0 * gram) * (1.0 / features), 0.0) + EPSILON
    inverse = lax.rsqrt(squared)
    pairs = jnp.where(same_token, squared * inverse, 0.0)
    coeff = jnp.where(same_token & ~same_row, inverse, 0.0).astype(BF16)
    coeff_sum = jnp.sum(coeff.astype(F32), axis=1, keepdims=True)
    combined = jnp.dot(coeff, forecast, preferred_element_type=F32)
    values = forecast.astype(F32)
    apart = (
        values.reshape(members, tokens, features) - targets.astype(F32)[None]
    )
    squares = jnp.sum(apart * apart, axis=-1, keepdims=True) * (1.0 / features) + EPSILON
    inverse_spread = lax.rsqrt(squares)
    from_others = (coeff_sum * values - combined).reshape(members, tokens, features)
    gradient = scale[None] * (apart * inverse_spread - from_others * (1.0 / members))
    spread = jnp.sum(squares * inverse_spread, axis=0) * (1.0 / members)
    pair_sum = jnp.sum(jnp.sum(pairs, axis=1, keepdims=True).reshape(members, tokens, 1), axis=0)
    energy = scale * (spread - pair_sum * (1.0 / (2.0 * members * members)))
    return gradient, energy


def member_kernel(
    token_count,
    noise_ref,
    latent_ref,
    targets_ref,
    weight_ref,
    total_ref,
    inlet_hbm,
    outlet_hbm,
    gradient_ref,
    energy_ref,
    inlet,
    outlet,
    in_sems,
    out_sems,
):
    members, tokens, features = noise_ref.shape
    piece_width = inlet.shape[1] // HIDDEN_PIECES
    first = pl.program_id(0) == 0

    def copies(piece):
        part = pl.ds(piece * piece_width, piece_width)
        return (
            pltpu.make_async_copy(inlet_hbm.at[:, part], inlet.at[:, part], in_sems.at[piece]),
            pltpu.make_async_copy(outlet_hbm.at[part, :], outlet.at[part, :], out_sems.at[piece]),
        )

    @pl.when(first)
    def _():
        for piece in range(HIDDEN_PIECES):
            for copy in copies(piece):
                copy.start()

    def hidden_piece(normed, piece):
        @pl.when(first)
        def _():
            for copy in copies(piece):
                copy.wait()

        part = pl.ds(piece * piece_width, piece_width)
        hidden = jax.nn.gelu(
            jnp.dot(normed, inlet[:, part], preferred_element_type=F32), approximate=True
        ).astype(BF16)
        return jnp.dot(hidden, outlet[part, :], preferred_element_type=F32)

    forecast = network(noise_ref[...], latent_ref[...], hidden_piece, HIDDEN_PIECES)
    scale = weight_ref[...] * token_count / total_ref[0:1, 0:1]
    gradient, energy = score(forecast, targets_ref[...], scale, members, tokens)
    gradient_ref[...] = gradient.astype(BF16)
    energy_ref[...] = energy


def scored(noise, latent, targets, area_weight, total, inlet, outlet, token_count):
    members, own, features = noise.shape
    hidden = inlet.shape[1]
    tokens = TOKENS_AT_ONCE
    flops = 2 * members * own * (2 * features * hidden + 2 * members * tokens * features)
    return pl.pallas_call(
        functools.partial(member_kernel, token_count),
        grid=(own // tokens,),
        in_specs=[
            pl.BlockSpec((members, tokens, features), lambda i: (0, i, 0)),
            pl.BlockSpec((tokens, features), lambda i: (i, 0)),
            pl.BlockSpec((tokens, features), lambda i: (i, 0)),
            pl.BlockSpec((tokens, 1), lambda i: (i, 0)),
            pl.BlockSpec((8, 128), lambda i: (0, 0)),
            pl.BlockSpec(memory_space=pl.ANY),
            pl.BlockSpec(memory_space=pl.ANY),
        ],
        out_specs=[
            pl.BlockSpec((members, tokens, features), lambda i: (0, i, 0)),
            pl.BlockSpec((tokens, 1), lambda i: (i, 0)),
        ],
        out_shape=[
            jax.ShapeDtypeStruct((members, own, features), BF16),
            jax.ShapeDtypeStruct((own, 1), F32),
        ],
        scratch_shapes=[
            pltpu.VMEM((features, hidden), BF16),
            pltpu.VMEM((hidden, features), BF16),
            pltpu.SemaphoreType.DMA((HIDDEN_PIECES,)),
            pltpu.SemaphoreType.DMA((HIDDEN_PIECES,)),
        ],
        compiler_params=pltpu.CompilerParams(vmem_limit_bytes=40 * 2**20),
        cost_estimate=pl.CostEstimate(
            flops=flops, bytes_accessed=4 * features * hidden, transcendentals=0
        ),
    )(noise, latent, targets, area_weight, total, inlet, outlet)


def on_device(
    analyses,
    owners,
    noise,
    targets,
    area_weight,
    enc_weight,
    sample_inlet_matrix,
    sample_outlet_matrix,
):
    members = lax.axis_size("member")
    _, region_rows, features = noise.shape
    own = region_rows // members
    here = lax.all_to_all(
        noise.reshape(members, own, features), "member", split_axis=0, concat_axis=0, tiled=True
    )
    total = total_weight(area_weight)
    control = control_rows(analyses, owners)
    latent = jnp.dot(control, enc_weight, preferred_element_type=F32).astype(BF16)
    gradient, energy = scored(
        here,
        latent,
        targets,
        area_weight[:, None],
        total,
        sample_inlet_matrix,
        sample_outlet_matrix,
        float(region_rows * lax.axis_size("region")),
    )
    back = lax.all_to_all(gradient, "member", split_axis=0, concat_axis=0, tiled=True)
    return back.reshape(1, region_rows, features), energy[:, 0]


def solution(mesh):
    return jax.shard_map(
        on_device,
        mesh=mesh,
        in_specs=(
            P("member", "region", None),
            P(),
            P("member", "region", None),
            P(("region", "member"), None),
            P(("region", "member")),
            P(),
            P(),
            P(),
        ),
        out_specs=(P("member", "region", None), P(("region", "member"))),
        check_vma=False,
    )
```

```python
import functools

import jax
import jax.numpy as jnp
from jax import lax
from jax.experimental import pallas as pl
from jax.experimental.pallas import tpu as pltpu
from jax.sharding import PartitionSpec as P

EPSILON = 1e-06
TOKENS_AT_ONCE = 16
HIDDEN_PIECES = 2
TAIL = 16
BF16 = jnp.bfloat16
F32 = jnp.float32

VMEM = pl.BlockSpec(memory_space=pltpu.VMEM)
SMEM = pl.BlockSpec(memory_space=pltpu.SMEM)
ANY = pl.BlockSpec(memory_space=pl.ANY)


def swap(value, axis, bit):
    size = lax.axis_size(axis)
    return lax.ppermute(value, axis, [(i, i ^ bit) for i in range(size)])


def local_call(kernel, out_shape, in_specs, flops=0, moved=0, scratch=(), limit=40):
    return pl.pallas_call(
        kernel,
        in_specs=in_specs,
        out_specs=[VMEM] * len(out_shape),
        out_shape=out_shape,
        scratch_shapes=list(scratch),
        compiler_params=pltpu.CompilerParams(vmem_limit_bytes=limit * 2**20),
        cost_estimate=pl.CostEstimate(flops=flops, bytes_accessed=moved, transcendentals=0),
    )


def weight_rows(total, features):
    high = total.astype(BF16).astype(F32)
    middle = (total - high).astype(BF16).astype(F32)
    low = total - high - middle
    row = lax.broadcasted_iota(jnp.int32, (TAIL, features), 0)
    picked = jnp.where(row == 0, high, jnp.where(row == 1, middle, jnp.where(row == 2, low, 0.0)))
    return picked.astype(BF16)


def weight_from(rows):
    return jnp.sum(rows[:, 0:128].astype(F32), axis=0, keepdims=True)[:, 0:1]


def lanes_kernel(lanes, owners, analyses, weight, *refs):
    outs, sems = refs[:lanes], refs[lanes]
    own = outs[0].shape[0] - TAIL
    features = outs[0].shape[1]
    me = lax.axis_index("member")
    lane = me % lanes
    block = jnp.int32(0)
    for b in range(owners.shape[0]):
        block = jnp.where(owners[b] == me, b, block)
    copies = []
    for k in range(lanes):
        start = pl.multiple_of((block * lanes + (lane ^ k)) * own, own)
        copies.append(
            pltpu.make_async_copy(
                analyses.at[0, pl.ds(start, own), :], outs[k].at[pl.ds(0, own), :], sems.at[k]
            )
        )
    for copy in copies:
        copy.start()
    total = jnp.sum(weight[...], axis=1, keepdims=True)
    rows = weight_rows(total, features)
    for k in range(lanes):
        outs[k][pl.ds(own, TAIL), :] = rows
    for copy in copies:
        copy.wait()


def blocks_kernel(lanes, blocks, owners, *refs):
    held, (keep, give, total_out) = refs[:lanes], refs[lanes:]
    own, features = keep.shape[1], keep.shape[2]
    me = lax.axis_index("member")
    lane, here = me % lanes, me // lanes

    def rows_of(block):
        place = (owners[block] % lanes) ^ lane
        rows = held[0][pl.ds(0, own), :]
        for k in range(1, lanes):
            rows = jnp.where(place == k, held[k][pl.ds(0, own), :], rows)
        return rows

    side = here % 2
    for j in range(blocks // 2):
        keep[j] = rows_of(2 * j + side)
        give[pl.ds(j * own, own), :] = rows_of(2 * j + 1 - side)
    total = weight_from(held[0][pl.ds(own, TAIL), :])
    for k in range(1, lanes):
        total = total + weight_from(held[k][pl.ds(own, TAIL), :])
    give[pl.ds(blocks // 2 * own, TAIL), :] = weight_rows(total, features)
    total_out[...] = jnp.broadcast_to(total, total_out.shape)


def merged(owners, lanes, here, bit, keep, got, j, own):
    block = j * (2 * bit) + here % (2 * bit)
    there = ((owners[block] // lanes) ^ here) // bit % 2
    return jnp.where(there == 1, got[pl.ds(j * own, own), :], keep[j])


def halve_kernel(lanes, bit, owners, keep, got, total, keep_out, give, total_out):
    count, own, features = keep.shape
    here = lax.axis_index("member") // lanes
    side = here // (2 * bit) % 2
    rows = [merged(owners, lanes, here, bit, keep, got, j, own) for j in range(count)]
    for j in range(count // 2):
        keep_out[j] = jnp.where(side == 1, rows[2 * j + 1], rows[2 * j])
        give[pl.ds(j * own, own), :] = jnp.where(side == 1, rows[2 * j], rows[2 * j + 1])
    summed = total[0:1, 0:1] + weight_from(got[pl.ds(count * own, TAIL), :])
    give[pl.ds(count // 2 * own, TAIL), :] = weight_rows(summed, features)
    total_out[...] = jnp.broadcast_to(summed, total_out.shape)


def column(row):
    size = row.shape[1]
    first = lax.broadcasted_iota(jnp.int32, (size, size), 0)
    second = lax.broadcasted_iota(jnp.int32, (size, size), 1)
    return jnp.sum(jnp.where(first == second, row, 0.0), axis=1, keepdims=True)


def encode_kernel(lanes, bit, count, owners, keep, got, total, weight, encoder, latent, scale):
    _, own, _ = keep.shape
    here = lax.axis_index("member") // lanes
    control = merged(owners, lanes, here, bit, keep, got, 0, own)
    latent[...] = jnp.dot(control, encoder[...], preferred_element_type=F32).astype(BF16)
    summed = total[0:1, 0:1] + weight_from(got[pl.ds(own, TAIL), :])
    scale[...] = column(weight[...]) * (count / summed)


def latent_and_scale(analyses, owners, weight, weight_across, encoder):
    members = lax.axis_size("member")
    _, rows, features = analyses.shape
    blocks = owners.shape[0]
    lanes, own = members // blocks, rows // members
    count = float(rows * lax.axis_size("region"))
    small = jax.ShapeDtypeStruct((8, 128), F32)

    def some(rows):
        return jax.ShapeDtypeStruct((rows, features), BF16)

    def kept(many):
        return jax.ShapeDtypeStruct((many, own, features), BF16)

    by_lane = local_call(
        functools.partial(lanes_kernel, lanes),
        [some(own + TAIL)] * lanes,
        [SMEM, ANY, VMEM],
        scratch=[pltpu.SemaphoreType.DMA((lanes,))],
        limit=8,
    )(owners, analyses, weight_across)
    by_lane = [by_lane[0]] + [swap(by_lane[k], "member", k) for k in range(1, lanes)]
    keep, give, total = local_call(
        functools.partial(blocks_kernel, lanes, blocks),
        [kept(blocks // 2), some(blocks // 2 * own + TAIL), small],
        [SMEM] + [VMEM] * lanes,
        limit=8,
    )(owners, *by_lane)
    bit = 1
    while 2 * bit < blocks:
        got = swap(give, "member", bit * lanes)
        many = keep.shape[0] // 2
        keep, give, total = local_call(
            functools.partial(halve_kernel, lanes, bit),
            [kept(many), some(many * own + TAIL), small],
            [SMEM] + [VMEM] * 3,
            limit=8,
        )(owners, keep, got, total)
        bit *= 2
    got = swap(give, "member", bit * lanes)
    return local_call(
        functools.partial(encode_kernel, lanes, bit, count),
        [some(own), jax.ShapeDtypeStruct((own, 1), F32)],
        [SMEM] + [VMEM] * 5,
        flops=2 * own * features * features,
        limit=8,
    )(owners, keep, got, total, weight, encoder)


def network(noise, latent, hidden_piece, pieces):
    members, tokens, features = noise.shape
    states = (noise.astype(F32) + latent.astype(F32)[None]).reshape(members * tokens, features)
    mean = jnp.sum(states * states, axis=-1, keepdims=True) * (1.0 / features)
    normed = (states * lax.rsqrt(mean + EPSILON)).astype(BF16)
    total = states
    for piece in range(pieces):
        total = total + hidden_piece(normed, piece)
    return total.astype(BF16)


def score(forecast, targets, scale, members, tokens):
    rows, features = forecast.shape
    gram = lax.dot_general(
        forecast, forecast, (((1,), (1,)), ((), ())), preferred_element_type=F32
    )
    first = lax.broadcasted_iota(jnp.int32, (rows, rows), 0)
    second = lax.broadcasted_iota(jnp.int32, (rows, rows), 1)
    same_row = first == second
    same_token = (first % tokens) == (second % tokens)
    on_diagonal = jnp.where(same_row, gram, 0.0)
    down = jnp.sum(on_diagonal, axis=1, keepdims=True)
    across = jnp.sum(on_diagonal, axis=0, keepdims=True)
    squared = jnp.maximum((down + across - 2.0 * gram) * (1.0 / features), 0.0) + EPSILON
    inverse = lax.rsqrt(squared)
    pairs = jnp.where(same_token, squared * inverse, 0.0)
    coeff = jnp.where(same_token & ~same_row, inverse, 0.0).astype(BF16)
    coeff_sum = jnp.sum(coeff.astype(F32), axis=1, keepdims=True)
    combined = jnp.dot(coeff, forecast, preferred_element_type=F32)
    values = forecast.astype(F32)
    apart = (
        values.reshape(members, tokens, features) - targets.astype(F32)[None]
    )
    squares = jnp.sum(apart * apart, axis=-1, keepdims=True) * (1.0 / features) + EPSILON
    inverse_spread = lax.rsqrt(squares)
    from_others = (coeff_sum * values - combined).reshape(members, tokens, features)
    gradient = scale[None] * (apart * inverse_spread - from_others * (1.0 / members))
    spread = jnp.sum(squares * inverse_spread, axis=0) * (1.0 / members)
    pair_sum = jnp.sum(jnp.sum(pairs, axis=1, keepdims=True).reshape(members, tokens, 1), axis=0)
    energy = scale * (spread - pair_sum * (1.0 / (2.0 * members * members)))
    return gradient, energy


def member_kernel(noise, latent, targets, scale, inlet, outlet, gradient_out, energy_out):
    members, own, features = noise.shape
    width = inlet.shape[1] // HIDDEN_PIECES

    def hidden_piece(normed, piece):
        part = slice(piece * width, (piece + 1) * width)
        hidden = jax.nn.gelu(
            jnp.dot(normed, inlet[:, part], preferred_element_type=F32), approximate=True
        ).astype(BF16)
        return jnp.dot(hidden, outlet[part, :], preferred_element_type=F32)

    forecast = network(noise[...], latent[...], hidden_piece, HIDDEN_PIECES)
    forecast = forecast.reshape(members, own, features)
    for first in range(0, own, TOKENS_AT_ONCE):
        here = slice(first, first + TOKENS_AT_ONCE)
        gradient, energy = score(
            forecast[:, here].reshape(members * TOKENS_AT_ONCE, features),
            targets[here, :],
            scale[here, :],
            members,
            TOKENS_AT_ONCE,
        )
        gradient_out[:, here, :] = gradient.astype(BF16)
        energy_out[here, :] = energy


def on_device(
    analyses,
    owners,
    noise,
    targets,
    area_weight,
    enc_weight,
    sample_inlet_matrix,
    sample_outlet_matrix,
):
    members = lax.axis_size("member")
    _, region_rows, features = noise.shape
    hidden = sample_inlet_matrix.shape[1]
    own = region_rows // members
    regions = lax.axis_size("region")
    weight_across = area_weight
    for bit in (1 << i for i in range(regions.bit_length() - 1)):
        weight_across = weight_across + swap(weight_across, "region", bit)
    here = lax.all_to_all(
        noise.reshape(members, own, features), "member", split_axis=0, concat_axis=0, tiled=True
    )
    latent, scale = latent_and_scale(
        analyses, owners, area_weight[None], weight_across[None], enc_weight
    )
    gradient, energy = local_call(
        member_kernel,
        [
            jax.ShapeDtypeStruct((members, own, features), BF16),
            jax.ShapeDtypeStruct((own, 1), F32),
        ],
        [VMEM] * 6,
        flops=4 * members * own * features * (hidden + members),
        moved=4 * features * hidden,
    )(here, latent, targets, scale, sample_inlet_matrix, sample_outlet_matrix)
    back = lax.all_to_all(gradient, "member", split_axis=0, concat_axis=0, tiled=True)
    return back.reshape(1, region_rows, features), energy[:, 0]


def solution(mesh):
    return jax.shard_map(
        on_device,
        mesh=mesh,
        in_specs=(
            P("member", "region", None),
            P(),
            P("member", "region", None),
            P(("region", "member"), None),
            P(("region", "member")),
            P(),
            P(),
            P(),
        ),
        out_specs=(P("member", "region", None), P(("region", "member"))),
        check_vma=False,
    )
```

```python
import functools

import jax
import jax.numpy as jnp
from jax import lax
from jax.experimental import pallas as pl
from jax.experimental.pallas import tpu as pltpu
from jax.sharding import PartitionSpec as P

EPSILON = 1e-06
TOKENS_AT_ONCE = 16
HIDDEN_PIECES = 4
NETWORK_LIMIT = 50
FIRST_LIMIT = 54
TAIL = 16
BF16 = jnp.bfloat16
F32 = jnp.float32

VMEM = pl.BlockSpec(memory_space=pltpu.VMEM)
SMEM = pl.BlockSpec(memory_space=pltpu.SMEM)
HBM = pl.BlockSpec(memory_space=pltpu.HBM)


def swap(value, axis, bit):
    size = lax.axis_size(axis)
    return lax.ppermute(value, axis, [(i, i ^ bit) for i in range(size)])


def transposed(value):
    return lax.all_to_all(value, "member", split_axis=0, concat_axis=0, tiled=True)


def local_call(kernel, out_shape, in_specs, flops=0, moved=0, scratch=(), limit=40):
    return pl.pallas_call(
        kernel,
        in_specs=in_specs,
        out_specs=[VMEM] * len(out_shape),
        out_shape=out_shape,
        scratch_shapes=list(scratch),
        compiler_params=pltpu.CompilerParams(vmem_limit_bytes=limit * 2**20),
        cost_estimate=pl.CostEstimate(flops=flops, bytes_accessed=moved, transcendentals=0),
    )


def weight_rows(total, features):
    high = total.astype(BF16).astype(F32)
    middle = (total - high).astype(BF16).astype(F32)
    low = total - high - middle
    row = lax.broadcasted_iota(jnp.int32, (TAIL, features), 0)
    picked = jnp.where(row == 0, high, jnp.where(row == 1, middle, jnp.where(row == 2, low, 0.0)))
    return picked.astype(BF16)


def weight_from(rows):
    return jnp.sum(rows[:, 0:128].astype(F32), axis=0, keepdims=True)[:, 0:1]


def first_kernel(lanes, chunks, owners, analyses, noise, weight, *refs):
    rows_out, noise_out = refs[:lanes], refs[lanes : lanes + chunks]
    row_sems, noise_sems = refs[lanes + chunks :]
    own, features = rows_out[0].shape[0] - TAIL, rows_out[0].shape[1]
    me = lax.axis_index("member")
    lane = me % lanes
    block = jnp.int32(0)
    for b in range(owners.shape[0]):
        block = jnp.where(owners[b] == me, b, block)
    copies = []
    for k in range(lanes):
        start = pl.multiple_of((block * lanes + (lane ^ k)) * own, own)
        copies.append(
            pltpu.make_async_copy(
                analyses.at[0, pl.ds(start, own), :],
                rows_out[k].at[pl.ds(0, own), :],
                row_sems.at[k],
            )
        )
    for i in range(chunks):
        tokens = noise_out[i].shape[1]
        copies.append(
            pltpu.make_async_copy(
                noise.at[:, pl.ds(i * tokens, tokens), :], noise_out[i], noise_sems.at[i]
            )
        )
    for copy in copies:
        copy.start()
    rows = weight_rows(jnp.sum(weight[...], axis=1, keepdims=True), features)
    for k in range(lanes):
        rows_out[k][pl.ds(own, TAIL), :] = rows
    for copy in copies:
        copy.wait()


def planes_kernel(lanes, owners, *refs):
    held, outs = refs[:lanes], refs[lanes:]
    own, features = outs[0].shape[0] - TAIL, outs[0].shape[1]
    me = lax.axis_index("member")
    lane, plane = me % lanes, me // lanes
    total = weight_from(held[0][pl.ds(own, TAIL), :])
    for k in range(1, lanes):
        total = total + weight_from(held[k][pl.ds(own, TAIL), :])
    tail = weight_rows(total, features)
    for j in range(len(outs)):
        place = (owners[plane ^ j] % lanes) ^ lane
        rows = held[0][pl.ds(0, own), :]
        for k in range(1, lanes):
            rows = jnp.where(place == k, held[k][pl.ds(0, own), :], rows)
        outs[j][pl.ds(0, own), :] = rows
        outs[j][pl.ds(own, TAIL), :] = tail


def encode_kernel(lanes, owners, encoder, *refs):
    held, (latent, total_out) = refs[:-2], refs[-2:]
    own = latent.shape[0]
    plane = lax.axis_index("member") // lanes
    place = (owners[plane] // lanes) ^ plane
    control = held[0][pl.ds(0, own), :]
    total = weight_from(held[0][pl.ds(own, TAIL), :])
    for k in range(1, len(held)):
        control = jnp.where(place == k, held[k][pl.ds(0, own), :], control)
        total = total + weight_from(held[k][pl.ds(own, TAIL), :])
    latent[...] = jnp.dot(control, encoder[...], preferred_element_type=F32).astype(BF16)
    total_out[...] = jnp.broadcast_to(total, total_out.shape)


def column(row):
    size = row.shape[1]
    first = lax.broadcasted_iota(jnp.int32, (size, size), 0)
    second = lax.broadcasted_iota(jnp.int32, (size, size), 1)
    return jnp.sum(jnp.where(first == second, row, 0.0), axis=1, keepdims=True)


def network(noise, latent, hidden_piece, pieces):
    members, tokens, features = noise.shape
    states = (noise.astype(F32) + latent.astype(F32)[None]).reshape(members * tokens, features)
    mean = jnp.sum(states * states, axis=-1, keepdims=True) * (1.0 / features)
    normed = (states * lax.rsqrt(mean + EPSILON)).astype(BF16)
    total = states
    for piece in range(pieces):
        total = total + hidden_piece(normed, piece)
    return total.astype(BF16)


def score(forecast, targets, scale, members, tokens):
    rows, features = forecast.shape
    gram = lax.dot_general(
        forecast, forecast, (((1,), (1,)), ((), ())), preferred_element_type=F32
    )
    first = lax.broadcasted_iota(jnp.int32, (rows, rows), 0)
    second = lax.broadcasted_iota(jnp.int32, (rows, rows), 1)
    same_row = first == second
    same_token = (first % tokens) == (second % tokens)
    on_diagonal = jnp.where(same_row, gram, 0.0)
    down = jnp.sum(on_diagonal, axis=1, keepdims=True)
    across = jnp.sum(on_diagonal, axis=0, keepdims=True)
    squared = jnp.maximum((down + across - 2.0 * gram) * (1.0 / features), 0.0) + EPSILON
    inverse = lax.rsqrt(squared)
    pairs = jnp.where(same_token, squared * inverse, 0.0)
    coeff = jnp.where(same_token & ~same_row, inverse, 0.0).astype(BF16)
    coeff_sum = jnp.sum(coeff.astype(F32), axis=1, keepdims=True)
    combined = jnp.dot(coeff, forecast, preferred_element_type=F32)
    values = forecast.astype(F32)
    apart = (
        values.reshape(members, tokens, features) - targets.astype(F32)[None]
    )
    squares = jnp.sum(apart * apart, axis=-1, keepdims=True) * (1.0 / features) + EPSILON
    inverse_spread = lax.rsqrt(squares)
    from_others = (coeff_sum * values - combined).reshape(members, tokens, features)
    gradient = scale[None] * (apart * inverse_spread - from_others * (1.0 / members))
    spread = jnp.sum(squares * inverse_spread, axis=0) * (1.0 / members)
    pair_sum = jnp.sum(jnp.sum(pairs, axis=1, keepdims=True).reshape(members, tokens, 1), axis=0)
    energy = scale * (spread - pair_sum * (1.0 / (2.0 * members * members)))
    return gradient, energy


def network_kernel(
    chunk, noise, latent, inlet_hbm, outlet_hbm, forecast_out, inlet, outlet, inlet_sems, outlet_sems
):
    members, tokens, features = noise.shape
    width = inlet.shape[1] // HIDDEN_PIECES
    copies = []
    for piece in range(HIDDEN_PIECES):
        part = pl.ds(piece * width, width)
        copies.append(
            (
                pltpu.make_async_copy(
                    inlet_hbm.at[:, part], inlet.at[:, part], inlet_sems.at[piece]
                ),
                pltpu.make_async_copy(
                    outlet_hbm.at[part, :], outlet.at[part, :], outlet_sems.at[piece]
                ),
            )
        )
    for into, out_of in copies:
        into.start()
        out_of.start()

    def hidden_piece(normed, piece):
        part = slice(piece * width, (piece + 1) * width)
        copies[piece][0].wait()
        hidden = jax.nn.gelu(
            jnp.dot(normed, inlet[:, part], preferred_element_type=F32), approximate=True
        ).astype(BF16)
        copies[piece][1].wait()
        return jnp.dot(hidden, outlet[part, :], preferred_element_type=F32)

    here = slice(chunk * tokens, (chunk + 1) * tokens)
    forecast_out[...] = network(noise[...], latent[here, :], hidden_piece, HIDDEN_PIECES)


def scored(chunk, members, count, forecast, targets, weight, total):
    tokens = forecast.shape[0] // members
    here = slice(chunk * tokens, (chunk + 1) * tokens)
    scale = column(weight[...])[here, :] * (count / total[0:1, 0:1])
    gradient, energy = score(forecast[...], targets[here, :], scale, members, tokens)
    return gradient.astype(BF16), energy


def whole_score_kernel(chunk, count, forecast, targets, weight, total, gradient_out, energy_out):
    gradient, energy = scored(
        chunk, gradient_out.shape[0], count, forecast, targets, weight, total
    )
    gradient_out[...] = gradient
    energy_out[...] = energy


def split_score_kernel(
    chunk, count, forecast, targets, weight, total, keep, give, energy_out, gradient
):
    values, energy = scored(chunk, gradient.shape[0], count, forecast, targets, weight, total)
    gradient[...] = values
    energy_out[...] = energy
    me = lax.axis_index("member")
    for k in range(keep.shape[0]):
        keep[k] = gradient[me ^ (2 * k)]
        give[k] = gradient[me ^ (2 * k + 1)]


def pack_kernel(keep, got, *outs):
    for k, out in enumerate(outs):
        out[0] = keep[k + 1]
        out[1] = got[k + 1]


def finish_kernel(chips, own, *refs):
    *inputs, result, sems = refs
    back = inputs[-1]
    tokens = back.shape[1]
    chunk = own // tokens - 1
    me = lax.axis_index("member")
    copies = []

    def put(source, device, chunk):
        start = pl.multiple_of(device * own + chunk * tokens, tokens)
        copies.append(
            pltpu.make_async_copy(
                source, result.at[0, pl.ds(start, tokens), :], sems.at[len(copies)]
            )
        )

    for device in range(back.shape[0]):
        put(back.at[device], device, chunk)
    if chunk:
        keep, got = inputs[:2]
        put(keep.at[0], me, 0)
        put(got.at[0], me ^ 1, 0)
        for k in range(1, chips):
            put(inputs[k + 1].at[0], me ^ (2 * k), 0)
            put(inputs[k + 1].at[1], me ^ (2 * k + 1), 0)
    for copy in copies:
        copy.start()
    for copy in copies:
        copy.wait()


def on_device(
    analyses,
    owners,
    noise,
    targets,
    area_weight,
    enc_weight,
    sample_inlet_matrix,
    sample_outlet_matrix,
):
    members = lax.axis_size("member")
    regions = lax.axis_size("region")
    _, region_rows, features = noise.shape
    hidden = sample_inlet_matrix.shape[1]
    blocks = owners.shape[0]
    lanes = members // blocks
    chips = members // 2
    own = region_rows // members
    chunks = min(2, own // TOKENS_AT_ONCE)
    tokens = own // chunks
    count = float(region_rows * regions)
    weight = area_weight[None]

    def rows(many):
        return jax.ShapeDtypeStruct((many, features), BF16)

    def stack(many):
        return jax.ShapeDtypeStruct((many, tokens, features), BF16)

    small = jax.ShapeDtypeStruct((8, 128), F32)
    energies = jax.ShapeDtypeStruct((tokens, 1), F32)

    first = local_call(
        functools.partial(first_kernel, lanes, chunks),
        [rows(own + TAIL)] * lanes + [stack(members)] * chunks,
        [SMEM, HBM, HBM, VMEM],
        scratch=[pltpu.SemaphoreType.DMA((lanes,)), pltpu.SemaphoreType.DMA((chunks,))],
        limit=FIRST_LIMIT,
    )(owners, analyses, noise.reshape(members, own, features), weight)
    by_lane = [first[0]] + [swap(first[k], "member", k) for k in range(1, lanes)]
    parts = list(first[lanes:])
    parts[0], *by_lane = lax.optimization_barrier((parts[0], *by_lane))
    noises = [transposed(parts[0])]
    planes = local_call(
        functools.partial(planes_kernel, lanes),
        [rows(own + TAIL)] * blocks,
        [SMEM] + [VMEM] * lanes,
        limit=8,
    )(owners, *by_lane)
    by_plane = [planes[0]] + [swap(planes[k], "member", k * lanes) for k in range(1, blocks)]
    latent, total = local_call(
        functools.partial(encode_kernel, lanes),
        [rows(own), small],
        [SMEM] + [VMEM] * (1 + blocks),
        flops=2 * own * features * features,
        limit=8,
    )(owners, enc_weight, *by_plane)
    for part in parts[1:]:
        noises[-1], latent, part = lax.optimization_barrier((noises[-1], latent, part))
        noises.append(transposed(part))
    for bit in (1 << i for i in range(regions.bit_length() - 1)):
        total = total + swap(total, "region", bit)

    def forecast_of(chunk):
        return local_call(
            functools.partial(network_kernel, chunk),
            [rows(members * tokens)],
            [VMEM, VMEM, HBM, HBM],
            flops=4 * members * tokens * features * hidden,
            scratch=[
                pltpu.VMEM((features, hidden), BF16),
                pltpu.VMEM((hidden, features), BF16),
                pltpu.SemaphoreType.DMA((HIDDEN_PIECES,)),
                pltpu.SemaphoreType.DMA((HIDDEN_PIECES,)),
            ],
            limit=NETWORK_LIMIT,
        )(noises[chunk], latent, sample_inlet_matrix, sample_outlet_matrix)[0]

    energy, returned = [], []
    flops = 4 * members * tokens * features * members * tokens
    for chunk in range(chunks - 1):
        keep, give, part = local_call(
            functools.partial(split_score_kernel, chunk, count),
            [stack(chips), stack(chips), energies],
            [VMEM] * 4,
            flops=flops,
            scratch=[pltpu.VMEM((members, tokens, features), BF16)],
            limit=24,
        )(forecast_of(chunk), targets, weight, total)
        energy.append(part)
        got = swap(give, "member", 1)
        packed = local_call(pack_kernel, [stack(2)] * (chips - 1), [VMEM] * 2, limit=8)(keep, got)
        noises[chunk + 1], packed = lax.optimization_barrier((noises[chunk + 1], packed))
        returned = [keep, got] + [
            swap(packed[k - 1], "member", 2 * k) for k in range(1, chips)
        ]
    gradient, part = local_call(
        functools.partial(whole_score_kernel, chunks - 1, count),
        [stack(members), energies],
        [VMEM] * 4,
        flops=flops,
        limit=24,
    )(forecast_of(chunks - 1), targets, weight, total)
    energy.append(part)
    gradient, *returned = lax.optimization_barrier((gradient, *returned))
    back = transposed(gradient)
    member_grad = pl.pallas_call(
        functools.partial(finish_kernel, chips, own),
        in_specs=[VMEM] * (len(returned) + 1),
        out_specs=HBM,
        out_shape=jax.ShapeDtypeStruct((1, region_rows, features), BF16),
        scratch_shapes=[pltpu.SemaphoreType.DMA((members * chunks,))],
        compiler_params=pltpu.CompilerParams(vmem_limit_bytes=8 * 2**20),
    )(*returned, back)
    return member_grad, jnp.concatenate(energy, axis=0)[:, 0]


def solution(mesh):
    return jax.shard_map(
        on_device,
        mesh=mesh,
        in_specs=(
            P("member", "region", None),
            P(),
            P("member", "region", None),
            P(("region", "member"), None),
            P(("region", "member")),
            P(),
            P(),
            P(),
        ),
        out_specs=(P("member", "region", None), P(("region", "member"))),
        check_vma=False,
    )
```

```python
import functools

import jax
import jax.numpy as jnp
from jax import lax
from jax.experimental import pallas as pl
from jax.experimental.pallas import tpu as pltpu
from jax.sharding import PartitionSpec as P

EPSILON = 1e-06
TOKENS_AT_ONCE = 16
HIDDEN_PIECES = 4
NETWORK_LIMIT = 50
ROWS_LIMIT = 53
BF16 = jnp.bfloat16
F32 = jnp.float32

VMEM = pl.BlockSpec(memory_space=pltpu.VMEM)
SMEM = pl.BlockSpec(memory_space=pltpu.SMEM)
HBM = pl.BlockSpec(memory_space=pltpu.HBM)


def swap(value, axis, bit):
    size = lax.axis_size(axis)
    return lax.ppermute(value, axis, [(i, i ^ bit) for i in range(size)])


def bits_of(size):
    return [1 << i for i in range(size.bit_length() - 1)]


def transposed(value):
    return lax.all_to_all(value, "member", split_axis=0, concat_axis=0, tiled=True)


def local_call(kernel, out_shape, in_specs, flops=0, moved=0, scratch=(), limit=40):
    return pl.pallas_call(
        kernel,
        in_specs=in_specs,
        out_specs=[VMEM] * len(out_shape),
        out_shape=out_shape,
        scratch_shapes=list(scratch),
        compiler_params=pltpu.CompilerParams(vmem_limit_bytes=limit * 2**20),
        cost_estimate=pl.CostEstimate(flops=flops, bytes_accessed=moved, transcendentals=0),
    )


def rows_kernel(lanes, owners, analyses, *refs):
    outs, sems = refs[:lanes], refs[lanes]
    own = outs[0].shape[0]
    me = lax.axis_index("member")
    lane = me % lanes
    block = jnp.int32(0)
    for b in range(owners.shape[0]):
        block = jnp.where(owners[b] == me, b, block)
    copies = []
    for k in range(lanes):
        start = pl.multiple_of((block * lanes + (lane ^ k)) * own, own)
        copies.append(
            pltpu.make_async_copy(analyses.at[0, pl.ds(start, own), :], outs[k], sems.at[k])
        )
    for copy in copies:
        copy.start()
    for copy in copies:
        copy.wait()


def blocks_kernel(lanes, owners, *refs):
    held, (keep, give) = refs[:lanes], refs[lanes:]
    me = lax.axis_index("member")
    lane, plane = me % lanes, me // lanes

    def rows_of(block):
        place = (owners[block] % lanes) ^ lane
        rows = held[0][...]
        for k in range(1, lanes):
            rows = jnp.where(place == k, held[k][...], rows)
        return rows

    side = plane % 2
    for j in range(keep.shape[0]):
        keep[j] = rows_of(2 * j + side)
        give[j] = rows_of(2 * j + 1 - side)


def merged(lanes, owners, plane, bit, keep, got, j):
    block = j * (2 * bit) + plane % (2 * bit)
    there = ((owners[block] // lanes) ^ plane) // bit % 2
    return jnp.where(there == 1, got[j], keep[j])


def halve_kernel(lanes, bit, owners, keep, got, keep_out, give):
    plane = lax.axis_index("member") // lanes
    side = plane // (2 * bit) % 2
    rows = [merged(lanes, owners, plane, bit, keep, got, j) for j in range(keep.shape[0])]
    for j in range(keep_out.shape[0]):
        keep_out[j] = jnp.where(side == 1, rows[2 * j + 1], rows[2 * j])
        give[j] = jnp.where(side == 1, rows[2 * j], rows[2 * j + 1])


def encode_kernel(lanes, bit, owners, keep, got, encoder, latent):
    plane = lax.axis_index("member") // lanes
    control = merged(lanes, owners, plane, bit, keep, got, 0)
    latent[...] = jnp.dot(control, encoder[...], preferred_element_type=F32).astype(BF16)


def latent_rows(analyses, owners, encoder):
    members = lax.axis_size("member")
    _, rows, features = analyses.shape
    blocks = owners.shape[0]
    lanes, own = members // blocks, rows // members

    def kept(many):
        return jax.ShapeDtypeStruct((many, own, features), BF16)

    row = jax.ShapeDtypeStruct((own, features), BF16)
    by_lane = local_call(
        functools.partial(rows_kernel, lanes),
        [row] * lanes,
        [SMEM, HBM],
        scratch=[pltpu.SemaphoreType.DMA((lanes,))],
        limit=ROWS_LIMIT,
    )(owners, analyses)
    by_lane = [by_lane[0]] + [swap(by_lane[k], "member", k) for k in range(1, lanes)]
    keep, give = local_call(
        functools.partial(blocks_kernel, lanes),
        [kept(blocks // 2)] * 2,
        [SMEM] + [VMEM] * lanes,
        limit=8,
    )(owners, *by_lane)
    bit = 1
    while 2 * bit < blocks:
        got = swap(give, "member", bit * lanes)
        keep, give = local_call(
            functools.partial(halve_kernel, lanes, bit),
            [kept(keep.shape[0] // 2)] * 2,
            [SMEM] + [VMEM] * 2,
            limit=8,
        )(owners, keep, got)
        bit *= 2
    got = swap(give, "member", bit * lanes)
    return local_call(
        functools.partial(encode_kernel, lanes, bit),
        [row],
        [SMEM] + [VMEM] * 3,
        flops=2 * own * features * features,
        limit=8,
    )(owners, keep, got, encoder)[0]


def column(row):
    size = row.shape[1]
    first = lax.broadcasted_iota(jnp.int32, (size, size), 0)
    second = lax.broadcasted_iota(jnp.int32, (size, size), 1)
    return jnp.sum(jnp.where(first == second, row, 0.0), axis=1, keepdims=True)


def network(noise, latent, hidden_piece, pieces):
    members, tokens, features = noise.shape
    states = (noise.astype(F32) + latent.astype(F32)[None]).reshape(members * tokens, features)
    mean = jnp.sum(states * states, axis=-1, keepdims=True) * (1.0 / features)
    normed = (states * lax.rsqrt(mean + EPSILON)).astype(BF16)
    total = states
    for piece in range(pieces):
        total = total + hidden_piece(normed, piece)
    return total.astype(BF16)


def score(forecast, targets, scale, members, tokens):
    rows, features = forecast.shape
    gram = lax.dot_general(
        forecast, forecast, (((1,), (1,)), ((), ())), preferred_element_type=F32
    )
    first = lax.broadcasted_iota(jnp.int32, (rows, rows), 0)
    second = lax.broadcasted_iota(jnp.int32, (rows, rows), 1)
    same_row = first == second
    same_token = (first % tokens) == (second % tokens)
    on_diagonal = jnp.where(same_row, gram, 0.0)
    down = jnp.sum(on_diagonal, axis=1, keepdims=True)
    across = jnp.sum(on_diagonal, axis=0, keepdims=True)
    squared = jnp.maximum((down + across - 2.0 * gram) * (1.0 / features), 0.0) + EPSILON
    inverse = lax.rsqrt(squared)
    pairs = jnp.where(same_token, squared * inverse, 0.0)
    coeff = jnp.where(same_token & ~same_row, inverse, 0.0).astype(BF16)
    coeff_sum = jnp.sum(coeff.astype(F32), axis=1, keepdims=True)
    combined = jnp.dot(coeff, forecast, preferred_element_type=F32)
    values = forecast.astype(F32)
    apart = (
        values.reshape(members, tokens, features) - targets.astype(F32)[None]
    )
    squares = jnp.sum(apart * apart, axis=-1, keepdims=True) * (1.0 / features) + EPSILON
    inverse_spread = lax.rsqrt(squares)
    from_others = (coeff_sum * values - combined).reshape(members, tokens, features)
    gradient = scale[None] * (apart * inverse_spread - from_others * (1.0 / members))
    spread = jnp.sum(squares * inverse_spread, axis=0) * (1.0 / members)
    pair_sum = jnp.sum(jnp.sum(pairs, axis=1, keepdims=True).reshape(members, tokens, 1), axis=0)
    energy = scale * (spread - pair_sum * (1.0 / (2.0 * members * members)))
    return gradient, energy


def member_kernel(
    noise,
    latent,
    targets,
    weight,
    inlet_hbm,
    outlet_hbm,
    gradient_out,
    energy_out,
    inlet,
    outlet,
    inlet_sems,
    outlet_sems,
):
    members, own, features = noise.shape
    width = inlet.shape[1] // HIDDEN_PIECES
    copies = []
    for piece in range(HIDDEN_PIECES):
        part = pl.ds(piece * width, width)
        copies.append(
            (
                pltpu.make_async_copy(
                    inlet_hbm.at[:, part], inlet.at[:, part], inlet_sems.at[piece]
                ),
                pltpu.make_async_copy(
                    outlet_hbm.at[part, :], outlet.at[part, :], outlet_sems.at[piece]
                ),
            )
        )
    for into, out_of in copies:
        into.start()
        out_of.start()

    def hidden_piece(normed, piece):
        part = slice(piece * width, (piece + 1) * width)
        copies[piece][0].wait()
        hidden = jax.nn.gelu(
            jnp.dot(normed, inlet[:, part], preferred_element_type=F32), approximate=True
        ).astype(BF16)
        copies[piece][1].wait()
        return jnp.dot(hidden, outlet[part, :], preferred_element_type=F32)

    forecast = network(noise[...], latent[...], hidden_piece, HIDDEN_PIECES)
    forecast = forecast.reshape(members, own, features)
    scale = column(weight[...])
    for first in range(0, own, TOKENS_AT_ONCE):
        here = slice(first, first + TOKENS_AT_ONCE)
        gradient, energy = score(
            forecast[:, here].reshape(members * TOKENS_AT_ONCE, features),
            targets[here, :],
            scale[here, :],
            members,
            TOKENS_AT_ONCE,
        )
        gradient_out[:, here, :] = gradient.astype(BF16)
        energy_out[here, :] = energy


def on_device(
    analyses,
    owners,
    noise,
    targets,
    area_weight,
    enc_weight,
    sample_inlet_matrix,
    sample_outlet_matrix,
):
    members, regions = lax.axis_size("member"), lax.axis_size("region")
    _, region_rows, features = noise.shape
    hidden = sample_inlet_matrix.shape[1]
    own = region_rows // members
    here = transposed(noise.reshape(members, own, features))
    latent = latent_rows(analyses, owners, enc_weight)
    gradient, energy = local_call(
        member_kernel,
        [
            jax.ShapeDtypeStruct((members, own, features), BF16),
            jax.ShapeDtypeStruct((own, 1), F32),
        ],
        [VMEM] * 4 + [HBM] * 2,
        flops=4 * members * own * features * (hidden + members),
        moved=4 * features * hidden,
        scratch=[
            pltpu.VMEM((features, hidden), BF16),
            pltpu.VMEM((hidden, features), BF16),
            pltpu.SemaphoreType.DMA((HIDDEN_PIECES,)),
            pltpu.SemaphoreType.DMA((HIDDEN_PIECES,)),
        ],
        limit=NETWORK_LIMIT,
    )(here, latent, targets, area_weight[None], sample_inlet_matrix, sample_outlet_matrix)
    gradient, total = lax.optimization_barrier((gradient, area_weight))
    back = transposed(gradient)
    for bit in bits_of(members):
        total = total + swap(total, "member", bit)
    for bit in bits_of(regions):
        total = total + swap(total, "region", bit)
    factor = float(region_rows * regions) / jnp.sum(total)
    member_grad = (back.astype(F32) * factor).astype(BF16).reshape(1, region_rows, features)
    return member_grad, energy[:, 0] * factor


def solution(mesh):
    return jax.shard_map(
        on_device,
        mesh=mesh,
        in_specs=(
            P("member", "region", None),
            P(),
            P("member", "region", None),
            P(("region", "member"), None),
            P(("region", "member")),
            P(),
            P(),
            P(),
        ),
        out_specs=(P("member", "region", None), P(("region", "member"))),
        check_vma=False,
    )
```

```python
import functools

import jax
import jax.numpy as jnp
from jax import lax
from jax.experimental import pallas as pl
from jax.experimental.pallas import tpu as pltpu
from jax.sharding import PartitionSpec as P

EPSILON = 1e-06
TOKENS_AT_ONCE = 16
HIDDEN_PIECES = 4
NETWORK_LIMIT = 50
ROWS_LIMIT = 53
BF16 = jnp.bfloat16
F32 = jnp.float32

VMEM = pl.BlockSpec(memory_space=pltpu.VMEM)
SMEM = pl.BlockSpec(memory_space=pltpu.SMEM)
HBM = pl.BlockSpec(memory_space=pltpu.HBM)


def swap(value, axis, bit):
    size = lax.axis_size(axis)
    return lax.ppermute(value, axis, [(i, i ^ bit) for i in range(size)])


def bits_of(size):
    return [1 << i for i in range(size.bit_length() - 1)]


def transposed(value):
    return lax.all_to_all(value, "member", split_axis=0, concat_axis=0, tiled=True)


def local_call(kernel, out_shape, in_specs, flops=0, moved=0, scratch=(), limit=40):
    return pl.pallas_call(
        kernel,
        in_specs=in_specs,
        out_specs=[VMEM] * len(out_shape),
        out_shape=out_shape,
        scratch_shapes=list(scratch),
        compiler_params=pltpu.CompilerParams(vmem_limit_bytes=limit * 2**20),
        cost_estimate=pl.CostEstimate(flops=flops, bytes_accessed=moved, transcendentals=0),
    )


def rows_kernel(lanes, owners, analyses, *refs):
    outs, sems = refs[:lanes], refs[lanes]
    own = outs[0].shape[0]
    me = lax.axis_index("member")
    lane = me % lanes
    block = jnp.int32(0)
    for b in range(owners.shape[0]):
        block = jnp.where(owners[b] == me, b, block)
    copies = []
    for k in range(lanes):
        start = pl.multiple_of((block * lanes + (lane ^ k)) * own, own)
        copies.append(
            pltpu.make_async_copy(analyses.at[0, pl.ds(start, own), :], outs[k], sems.at[k])
        )
    for copy in copies:
        copy.start()
    for copy in copies:
        copy.wait()


def blocks_kernel(lanes, owners, *refs):
    held, (keep, give) = refs[:lanes], refs[lanes:]
    me = lax.axis_index("member")
    lane, plane = me % lanes, me // lanes

    def rows_of(block):
        place = (owners[block] % lanes) ^ lane
        rows = held[0][...]
        for k in range(1, lanes):
            rows = jnp.where(place == k, held[k][...], rows)
        return rows

    side = plane % 2
    for j in range(keep.shape[0]):
        keep[j] = rows_of(2 * j + side)
        give[j] = rows_of(2 * j + 1 - side)


def merged(lanes, owners, plane, bit, keep, got, j):
    block = j * (2 * bit) + plane % (2 * bit)
    there = ((owners[block] // lanes) ^ plane) // bit % 2
    return jnp.where(there == 1, got[j], keep[j])


def halve_kernel(lanes, bit, owners, keep, got, keep_out, give):
    plane = lax.axis_index("member") // lanes
    side = plane // (2 * bit) % 2
    rows = [merged(lanes, owners, plane, bit, keep, got, j) for j in range(keep.shape[0])]
    for j in range(keep_out.shape[0]):
        keep_out[j] = jnp.where(side == 1, rows[2 * j + 1], rows[2 * j])
        give[j] = jnp.where(side == 1, rows[2 * j], rows[2 * j + 1])


def encode_kernel(lanes, bit, owners, keep, got, encoder, latent):
    plane = lax.axis_index("member") // lanes
    control = merged(lanes, owners, plane, bit, keep, got, 0)
    latent[...] = jnp.dot(control, encoder[...], preferred_element_type=F32).astype(BF16)


def summed(value, axis, bits):
    for bit in bits:
        value = value + swap(value, axis, bit)
    return value


def latent_rows(analyses, owners, encoder, weight):
    members = lax.axis_size("member")
    _, rows, features = analyses.shape
    blocks = owners.shape[0]
    lanes, own = members // blocks, rows // members

    def kept(many):
        return jax.ShapeDtypeStruct((many, own, features), BF16)

    row = jax.ShapeDtypeStruct((own, features), BF16)
    by_lane = local_call(
        functools.partial(rows_kernel, lanes),
        [row] * lanes,
        [SMEM, HBM],
        scratch=[pltpu.SemaphoreType.DMA((lanes,))],
        limit=ROWS_LIMIT,
    )(owners, analyses)
    by_lane = [by_lane[0]] + [swap(by_lane[k], "member", k) for k in range(1, lanes)]
    keep, give = local_call(
        functools.partial(blocks_kernel, lanes),
        [kept(blocks // 2)] * 2,
        [SMEM] + [VMEM] * lanes,
        limit=8,
    )(owners, *by_lane)
    bit = 1
    while 2 * bit < blocks:
        got = swap(give, "member", bit * lanes)
        if bit == 1:
            weight = summed(weight, "region", bits_of(lax.axis_size("region")))
            got, weight = lax.optimization_barrier((got, weight))
        keep, give = local_call(
            functools.partial(halve_kernel, lanes, bit),
            [kept(keep.shape[0] // 2)] * 2,
            [SMEM] + [VMEM] * 2,
            limit=8,
        )(owners, keep, got)
        bit *= 2
    got = swap(give, "member", bit * lanes)
    weight = summed(weight, "member", [1])
    got, weight = lax.optimization_barrier((got, weight))
    latent = local_call(
        functools.partial(encode_kernel, lanes, bit),
        [row],
        [SMEM] + [VMEM] * 3,
        flops=2 * own * features * features,
        limit=8,
    )(owners, keep, got, encoder)[0]
    return latent, weight


def column(row):
    size = row.shape[1]
    first = lax.broadcasted_iota(jnp.int32, (size, size), 0)
    second = lax.broadcasted_iota(jnp.int32, (size, size), 1)
    return jnp.sum(jnp.where(first == second, row, 0.0), axis=1, keepdims=True)


def network(noise, latent, hidden_piece, pieces):
    members, tokens, features = noise.shape
    states = (noise.astype(F32) + latent.astype(F32)[None]).reshape(members * tokens, features)
    mean = jnp.sum(states * states, axis=-1, keepdims=True) * (1.0 / features)
    normed = (states * lax.rsqrt(mean + EPSILON)).astype(BF16)
    total = states
    for piece in range(pieces):
        total = total + hidden_piece(normed, piece)
    return total.astype(BF16)


def score(forecast, targets, scale, members, tokens):
    rows, features = forecast.shape
    gram = lax.dot_general(
        forecast, forecast, (((1,), (1,)), ((), ())), preferred_element_type=F32
    )
    first = lax.broadcasted_iota(jnp.int32, (rows, rows), 0)
    second = lax.broadcasted_iota(jnp.int32, (rows, rows), 1)
    same_row = first == second
    same_token = (first % tokens) == (second % tokens)
    on_diagonal = jnp.where(same_row, gram, 0.0)
    down = jnp.sum(on_diagonal, axis=1, keepdims=True)
    across = jnp.sum(on_diagonal, axis=0, keepdims=True)
    squared = jnp.maximum((down + across - 2.0 * gram) * (1.0 / features), 0.0) + EPSILON
    inverse = lax.rsqrt(squared)
    pairs = jnp.where(same_token, squared * inverse, 0.0)
    coeff = jnp.where(same_token & ~same_row, inverse, 0.0).astype(BF16)
    coeff_sum = jnp.sum(coeff.astype(F32), axis=1, keepdims=True)
    combined = jnp.dot(coeff, forecast, preferred_element_type=F32)
    values = forecast.astype(F32)
    apart = (
        values.reshape(members, tokens, features) - targets.astype(F32)[None]
    )
    squares = jnp.sum(apart * apart, axis=-1, keepdims=True) * (1.0 / features) + EPSILON
    inverse_spread = lax.rsqrt(squares)
    from_others = (coeff_sum * values - combined).reshape(members, tokens, features)
    gradient = scale[None] * (apart * inverse_spread - from_others * (1.0 / members))
    spread = jnp.sum(squares * inverse_spread, axis=0) * (1.0 / members)
    pair_sum = jnp.sum(jnp.sum(pairs, axis=1, keepdims=True).reshape(members, tokens, 1), axis=0)
    energy = scale * (spread - pair_sum * (1.0 / (2.0 * members * members)))
    return gradient, energy


def member_kernel(
    noise,
    latent,
    targets,
    weight,
    inlet_hbm,
    outlet_hbm,
    gradient_out,
    energy_out,
    inlet,
    outlet,
    inlet_sems,
    outlet_sems,
):
    members, own, features = noise.shape
    width = inlet.shape[1] // HIDDEN_PIECES
    copies = []
    for piece in range(HIDDEN_PIECES):
        part = pl.ds(piece * width, width)
        copies.append(
            (
                pltpu.make_async_copy(
                    inlet_hbm.at[:, part], inlet.at[:, part], inlet_sems.at[piece]
                ),
                pltpu.make_async_copy(
                    outlet_hbm.at[part, :], outlet.at[part, :], outlet_sems.at[piece]
                ),
            )
        )

    def fetch(piece):
        for copy in copies[piece]:
            copy.start()

    fetch(0)

    def hidden_piece(normed, piece):
        part = slice(piece * width, (piece + 1) * width)
        copies[piece][0].wait()
        if piece + 1 < HIDDEN_PIECES:
            fetch(piece + 1)
        hidden = jax.nn.gelu(
            jnp.dot(normed, inlet[:, part], preferred_element_type=F32), approximate=True
        ).astype(BF16)
        copies[piece][1].wait()
        return jnp.dot(hidden, outlet[part, :], preferred_element_type=F32)

    forecast = network(noise[...], latent[...], hidden_piece, HIDDEN_PIECES)
    forecast = forecast.reshape(members, own, features)
    scale = column(weight[...])
    for first in range(0, own, TOKENS_AT_ONCE):
        here = slice(first, first + TOKENS_AT_ONCE)
        gradient, energy = score(
            forecast[:, here].reshape(members * TOKENS_AT_ONCE, features),
            targets[here, :],
            scale[here, :],
            members,
            TOKENS_AT_ONCE,
        )
        gradient_out[:, here, :] = gradient.astype(BF16)
        energy_out[here, :] = energy


def on_device(
    analyses,
    owners,
    noise,
    targets,
    area_weight,
    enc_weight,
    sample_inlet_matrix,
    sample_outlet_matrix,
):
    members, regions = lax.axis_size("member"), lax.axis_size("region")
    _, region_rows, features = noise.shape
    hidden = sample_inlet_matrix.shape[1]
    own = region_rows // members
    here = transposed(noise.reshape(members, own, features))
    latent, total = latent_rows(analyses, owners, enc_weight, area_weight)
    gradient, energy = local_call(
        member_kernel,
        [
            jax.ShapeDtypeStruct((members, own, features), BF16),
            jax.ShapeDtypeStruct((own, 1), F32),
        ],
        [VMEM] * 4 + [HBM] * 2,
        flops=4 * members * own * features * (hidden + members),
        moved=4 * features * hidden,
        scratch=[
            pltpu.VMEM((features, hidden), BF16),
            pltpu.VMEM((hidden, features), BF16),
            pltpu.SemaphoreType.DMA((HIDDEN_PIECES,)),
            pltpu.SemaphoreType.DMA((HIDDEN_PIECES,)),
        ],
        limit=NETWORK_LIMIT,
    )(here, latent, targets, area_weight[None], sample_inlet_matrix, sample_outlet_matrix)
    planes = members // owners.shape[0]
    total = summed(total, "member", [bit for bit in bits_of(members) if 1 < bit < planes])
    gradient, total = lax.optimization_barrier((gradient, total))
    back = transposed(gradient)
    total = summed(total, "member", [bit for bit in bits_of(members) if bit >= planes])
    factor = float(region_rows * regions) / jnp.sum(total)
    member_grad = (back.astype(F32) * factor).astype(BF16).reshape(1, region_rows, features)
    return member_grad, energy[:, 0] * factor


def solution(mesh):
    return jax.shard_map(
        on_device,
        mesh=mesh,
        in_specs=(
            P("member", "region", None),
            P(),
            P("member", "region", None),
            P(("region", "member"), None),
            P(("region", "member")),
            P(),
            P(),
            P(),
        ),
        out_specs=(P("member", "region", None), P(("region", "member"))),
        check_vma=False,
    )
```

```python
import functools

import jax
import jax.numpy as jnp
from jax import lax
from jax.experimental import pallas as pl
from jax.experimental.pallas import tpu as pltpu
from jax.sharding import PartitionSpec as P

EPSILON = 1e-06
TOKENS_AT_ONCE = 16
HIDDEN_PIECES = 2
INLET_PARTS = 2
ROWS_LIMIT = 53
NETWORK_LIMIT = 50
BF16 = jnp.bfloat16
F32 = jnp.float32

VMEM = pl.BlockSpec(memory_space=pltpu.VMEM)
SMEM = pl.BlockSpec(memory_space=pltpu.SMEM)
HBM = pl.BlockSpec(memory_space=pltpu.HBM)


def swap(value, axis, bit):
    size = lax.axis_size(axis)
    return lax.ppermute(value, axis, [(i, i ^ bit) for i in range(size)])


def bits_of(size):
    return [1 << i for i in range(size.bit_length() - 1)]


def transposed(value):
    return lax.all_to_all(value, "member", split_axis=0, concat_axis=0, tiled=True)


def local_call(kernel, out_shape, in_specs, flops=0, moved=0, scratch=(), limit=40):
    return pl.pallas_call(
        kernel,
        in_specs=in_specs,
        out_specs=[VMEM] * len(out_shape),
        out_shape=out_shape,
        scratch_shapes=list(scratch),
        compiler_params=pltpu.CompilerParams(vmem_limit_bytes=limit * 2**20),
        cost_estimate=pl.CostEstimate(flops=flops, bytes_accessed=moved, transcendentals=0),
    )


def rows_kernel(lanes, owners, analyses, weight, *refs):
    *outs, weight_out, sems = refs
    own = outs[0].shape[0]
    me = lax.axis_index("member")
    lane = me % lanes
    block = jnp.int32(0)
    for b in range(owners.shape[0]):
        block = jnp.where(owners[b] == me, b, block)
    copies = [
        pltpu.make_async_copy(weight, weight_out, sems.at[lanes]),
    ]
    for k in range(lanes):
        start = pl.multiple_of((block * lanes + (lane ^ k)) * own, own)
        copies.append(
            pltpu.make_async_copy(analyses.at[0, pl.ds(start, own), :], outs[k], sems.at[k])
        )
    for copy in copies:
        copy.start()
    for copy in copies:
        copy.wait()


def blocks_kernel(lanes, owners, *refs):
    held, (weight, across, keep, give, weight_out) = refs[:lanes], refs[lanes:]
    weight_out[...] = weight[...] + across[...]
    me = lax.axis_index("member")
    lane, plane = me % lanes, me // lanes

    def rows_of(block):
        place = (owners[block] % lanes) ^ lane
        rows = held[0][...]
        for k in range(1, lanes):
            rows = jnp.where(place == k, held[k][...], rows)
        return rows

    side = plane % 2
    for j in range(keep.shape[0]):
        keep[j] = rows_of(2 * j + side)
        give[j] = rows_of(2 * j + 1 - side)


def merged(lanes, owners, plane, bit, keep, got, j):
    block = j * (2 * bit) + plane % (2 * bit)
    there = ((owners[block] // lanes) ^ plane) // bit % 2
    return jnp.where(there == 1, got[j], keep[j])


def halve_kernel(lanes, bit, owners, keep, got, *refs):
    *weights, keep_out, give, weight_out = refs
    weight_out[...] = sum((ref[...] for ref in weights[1:]), weights[0][...])
    plane = lax.axis_index("member") // lanes
    side = plane // (2 * bit) % 2
    rows = [merged(lanes, owners, plane, bit, keep, got, j) for j in range(keep.shape[0])]
    for j in range(keep_out.shape[0]):
        keep_out[j] = jnp.where(side == 1, rows[2 * j + 1], rows[2 * j])
        give[j] = jnp.where(side == 1, rows[2 * j], rows[2 * j + 1])


def encode_kernel(lanes, bit, count, owners, keep, got, encoder, weight, *refs):
    *weights, latent, scale = refs
    plane = lax.axis_index("member") // lanes
    control = merged(lanes, owners, plane, bit, keep, got, 0)
    latent[...] = jnp.dot(control, encoder[...], preferred_element_type=F32).astype(BF16)
    total = jnp.sum(sum((ref[...] for ref in weights[1:]), weights[0][...]), keepdims=True)
    scale[...] = weight[...] * (count / total)


def prepared(analyses, owners, encoder, area_weight):
    members, regions = lax.axis_size("member"), lax.axis_size("region")
    _, rows, features = analyses.shape
    blocks = owners.shape[0]
    lanes, own = members // blocks, rows // members
    row = jax.ShapeDtypeStruct((own, features), BF16)
    line = jax.ShapeDtypeStruct((1, own), F32)

    def kept(many):
        return jax.ShapeDtypeStruct((many, own, features), BF16)

    *by_lane, own_weight = local_call(
        functools.partial(rows_kernel, lanes),
        [row] * lanes + [line],
        [SMEM] + [HBM] * 2,
        scratch=[pltpu.SemaphoreType.DMA((lanes + 1,))],
        limit=ROWS_LIMIT,
    )(owners, analyses, area_weight[None])
    by_lane = [by_lane[0]] + [swap(by_lane[k], "member", k) for k in range(1, lanes)]
    weight = own_weight
    for bit in bits_of(regions)[:-1]:
        weight = weight + swap(weight, "region", bit)
    across = swap(weight, "region", regions // 2)
    keep, give, weight = local_call(
        functools.partial(blocks_kernel, lanes),
        [kept(blocks // 2)] * 2 + [line],
        [SMEM] + [VMEM] * (lanes + 2),
        limit=8,
    )(owners, *by_lane, weight, across)
    weights = [weight] + [swap(weight, "member", k) for k in range(1, lanes)]
    bit = 1
    while 2 * bit < blocks:
        got = swap(give, "member", bit * lanes)
        keep, give, weight = local_call(
            functools.partial(halve_kernel, lanes, bit),
            [kept(keep.shape[0] // 2)] * 2 + [line],
            [SMEM] + [VMEM] * (2 + len(weights)),
            limit=8,
        )(owners, keep, got, *weights)
        weights = [weight]
        bit *= 2
    got = swap(give, "member", bit * lanes)
    weights = [weight] + [swap(weight, "member", k * lanes) for k in range(1, blocks)]
    latent, scale = local_call(
        functools.partial(encode_kernel, lanes, bit, float(rows * regions)),
        [row, line],
        [SMEM] + [VMEM] * (4 + len(weights)),
        flops=2 * own * features * features,
        limit=8,
    )(owners, keep, got, encoder, own_weight, *weights)
    return latent, scale


def column(row):
    size = row.shape[1]
    first = lax.broadcasted_iota(jnp.int32, (size, size), 0)
    second = lax.broadcasted_iota(jnp.int32, (size, size), 1)
    return jnp.sum(jnp.where(first == second, row, 0.0), axis=1, keepdims=True)


def network(noise, latent, hidden_piece, pieces):
    members, tokens, features = noise.shape
    states = (noise.astype(F32) + latent.astype(F32)[None]).reshape(members * tokens, features)
    mean = jnp.sum(states * states, axis=-1, keepdims=True) * (1.0 / features)
    normed = (states * lax.rsqrt(mean + EPSILON)).astype(BF16)
    total = states
    for piece in range(pieces):
        total = total + hidden_piece(normed, piece)
    return total.astype(BF16)


def score(forecast, targets, scale, members, tokens):
    rows, features = forecast.shape
    gram = lax.dot_general(
        forecast, forecast, (((1,), (1,)), ((), ())), preferred_element_type=F32
    )
    first = lax.broadcasted_iota(jnp.int32, (rows, rows), 0)
    second = lax.broadcasted_iota(jnp.int32, (rows, rows), 1)
    same_row = first == second
    same_token = (first % tokens) == (second % tokens)
    on_diagonal = jnp.where(same_row, gram, 0.0)
    down = jnp.sum(on_diagonal, axis=1, keepdims=True)
    across = jnp.sum(on_diagonal, axis=0, keepdims=True)
    squared = jnp.maximum((down + across - 2.0 * gram) * (1.0 / features), 0.0) + EPSILON
    inverse = lax.rsqrt(squared)
    pairs = jnp.where(same_token, squared * inverse, 0.0)
    coeff = jnp.where(same_token & ~same_row, inverse, 0.0).astype(BF16)
    coeff_sum = jnp.sum(coeff.astype(F32), axis=1, keepdims=True)
    combined = jnp.dot(coeff, forecast, preferred_element_type=F32)
    values = forecast.astype(F32)
    apart = (
        values.reshape(members, tokens, features) - targets.astype(F32)[None]
    )
    squares = jnp.sum(apart * apart, axis=-1, keepdims=True) * (1.0 / features) + EPSILON
    inverse_spread = lax.rsqrt(squares)
    from_others = (coeff_sum * values - combined).reshape(members, tokens, features)
    gradient = scale[None] * (apart * inverse_spread - from_others * (1.0 / members))
    spread = jnp.sum(squares * inverse_spread, axis=0) * (1.0 / members)
    pair_sum = jnp.sum(jnp.sum(pairs, axis=1, keepdims=True).reshape(members, tokens, 1), axis=0)
    energy = scale * (spread - pair_sum * (1.0 / (2.0 * members * members)))
    return gradient, energy


def member_kernel(
    noise,
    latent,
    scale,
    targets_hbm,
    inlet_hbm,
    outlet_hbm,
    gradient_out,
    energy_out,
    targets,
    inlet,
    outlet,
    hidden,
    sems,
):
    members, own, features = noise.shape
    width = inlet.shape[1] // HIDDEN_PIECES
    part = width // INLET_PARTS
    copies = []
    for piece in range(HIDDEN_PIECES):
        for i in range(INLET_PARTS):
            columns = pl.ds(piece * width + i * part, part)
            copies.append((inlet_hbm.at[:, columns], inlet.at[:, columns]))
        rows = pl.ds(piece * width, width)
        copies.append((outlet_hbm.at[rows, :], outlet.at[rows, :]))
    copies = [
        pltpu.make_async_copy(source, target, sems.at[i])
        for i, (source, target) in enumerate(copies)
    ]

    def arrived(i):
        copies[i].wait()
        if i + 2 < len(copies):
            copies[i + 2].start()

    aside = pltpu.make_async_copy(targets_hbm, targets, sems.at[len(copies)])
    for copy in (*copies[:2], aside):
        copy.start()

    def hidden_piece(normed, piece):
        for i in range(INLET_PARTS):
            arrived(piece * (INLET_PARTS + 1) + i)
            first = piece * width + i * part
            hidden[:, i * part : (i + 1) * part] = jax.nn.gelu(
                jnp.dot(normed, inlet[:, first : first + part], preferred_element_type=F32),
                approximate=True,
            ).astype(BF16)
        arrived(piece * (INLET_PARTS + 1) + INLET_PARTS)
        rows = slice(piece * width, (piece + 1) * width)
        return jnp.dot(hidden[...], outlet[rows, :], preferred_element_type=F32)

    forecast = network(noise[...], latent[...], hidden_piece, HIDDEN_PIECES)
    forecast = forecast.reshape(members, own, features)
    aside.wait()
    scales = column(scale[...])
    for first in range(0, own, TOKENS_AT_ONCE):
        here = slice(first, first + TOKENS_AT_ONCE)
        gradient, energy = score(
            forecast[:, here].reshape(members * TOKENS_AT_ONCE, features),
            targets[here, :],
            scales[here, :],
            members,
            TOKENS_AT_ONCE,
        )
        gradient_out[:, here, :] = gradient.astype(BF16)
        energy_out[here, :] = energy


def on_device(
    analyses,
    owners,
    noise,
    targets,
    area_weight,
    enc_weight,
    sample_inlet_matrix,
    sample_outlet_matrix,
):
    members, regions = lax.axis_size("member"), lax.axis_size("region")
    _, region_rows, features = noise.shape
    hidden = sample_inlet_matrix.shape[1]
    own = region_rows // members
    here = transposed(noise.reshape(members, own, features))
    latent, scale = prepared(analyses, owners, enc_weight, area_weight)
    gradient, energy = local_call(
        member_kernel,
        [
            jax.ShapeDtypeStruct((members, own, features), BF16),
            jax.ShapeDtypeStruct((own, 1), F32),
        ],
        [VMEM] * 3 + [HBM] * 3,
        flops=4 * members * own * features * (hidden + members),
        moved=4 * features * hidden,
        scratch=[
            pltpu.VMEM((own, features), BF16),
            pltpu.VMEM((features, hidden), BF16),
            pltpu.VMEM((hidden, features), BF16),
            pltpu.VMEM((members * own, hidden // HIDDEN_PIECES), BF16),
            pltpu.SemaphoreType.DMA((HIDDEN_PIECES * (INLET_PARTS + 1) + 1,)),
        ],
        limit=NETWORK_LIMIT,
    )(here, latent, scale, targets, sample_inlet_matrix, sample_outlet_matrix)
    back = transposed(gradient)
    return back.reshape(1, region_rows, features), energy[:, 0]


def solution(mesh):
    return jax.shard_map(
        on_device,
        mesh=mesh,
        in_specs=(
            P("member", "region", None),
            P(),
            P("member", "region", None),
            P(("region", "member"), None),
            P(("region", "member")),
            P(),
            P(),
            P(),
        ),
        out_specs=(P("member", "region", None), P(("region", "member"))),
        check_vma=False,
    )
```

```python
import functools

import jax
import jax.numpy as jnp
from jax import lax
from jax.experimental import pallas as pl
from jax.experimental.pallas import tpu as pltpu
from jax.sharding import PartitionSpec as P

EPSILON = 1e-06
TOKENS_AT_ONCE = 16
TAIL = 16
HIDDEN_PIECES = 2
INLET_PARTS = 2
ROWS_LIMIT = 53
NETWORK_LIMIT = 50
BF16 = jnp.bfloat16
F32 = jnp.float32

VMEM = pl.BlockSpec(memory_space=pltpu.VMEM)
SMEM = pl.BlockSpec(memory_space=pltpu.SMEM)
HBM = pl.BlockSpec(memory_space=pltpu.HBM)


def swap(value, axis, bit):
    size = lax.axis_size(axis)
    return lax.ppermute(value, axis, [(i, i ^ bit) for i in range(size)])


def bits_of(size):
    return [1 << i for i in range(size.bit_length() - 1)]


def transposed(value):
    return lax.all_to_all(value, "member", split_axis=0, concat_axis=0, tiled=True)


def local_call(kernel, out_shape, in_specs, flops=0, moved=0, scratch=(), limit=40):
    return pl.pallas_call(
        kernel,
        in_specs=in_specs,
        out_specs=[VMEM] * len(out_shape),
        out_shape=out_shape,
        scratch_shapes=list(scratch),
        compiler_params=pltpu.CompilerParams(vmem_limit_bytes=limit * 2**20),
        cost_estimate=pl.CostEstimate(flops=flops, bytes_accessed=moved, transcendentals=0),
    )


def rows_kernel(lanes, owners, analyses, weight, *refs):
    *outs, weight_out, sems = refs
    own = outs[0].shape[0]
    me = lax.axis_index("member")
    lane = me % lanes
    block = jnp.int32(0)
    for b in range(owners.shape[0]):
        block = jnp.where(owners[b] == me, b, block)
    copies = [
        pltpu.make_async_copy(weight, weight_out, sems.at[lanes]),
    ]
    for k in range(lanes):
        start = pl.multiple_of((block * lanes + (lane ^ k)) * own, own)
        copies.append(
            pltpu.make_async_copy(analyses.at[0, pl.ds(start, own), :], outs[k], sems.at[k])
        )
    for copy in copies:
        copy.start()
    for copy in copies:
        copy.wait()


def blocks_kernel(lanes, owners, *refs):
    held, (weight, across, keep, give, weight_out) = refs[:lanes], refs[lanes:]
    weight_out[...] = weight[...] + across[...]
    me = lax.axis_index("member")
    lane, plane = me % lanes, me // lanes

    def rows_of(block):
        place = (owners[block] % lanes) ^ lane
        rows = held[0][...]
        for k in range(1, lanes):
            rows = jnp.where(place == k, held[k][...], rows)
        return rows

    side = plane % 2
    for j in range(keep.shape[0]):
        keep[j] = rows_of(2 * j + side)
        give[j] = rows_of(2 * j + 1 - side)


def weight_rows(total, features):
    high = total.astype(BF16).astype(F32)
    middle = (total - high).astype(BF16).astype(F32)
    low = total - high - middle
    row = lax.broadcasted_iota(jnp.int32, (TAIL, features), 0)
    picked = jnp.where(row == 0, high, jnp.where(row == 1, middle, jnp.where(row == 2, low, 0.0)))
    return picked.astype(BF16)


def weight_from(rows):
    return jnp.sum(rows[:, 0:128].astype(F32), axis=0, keepdims=True)


def merged(lanes, owners, plane, bit, keep, got, j):
    block = j * (2 * bit) + plane % (2 * bit)
    there = ((owners[block] // lanes) ^ plane) // bit % 2
    return jnp.where(there == 1, got[j], keep[j])


def halve_kernel(lanes, bit, owners, keep, got, *refs):
    *weights, keep_out, give, weight_out = refs
    own, features = keep.shape[1], keep.shape[2]
    total = jnp.sum(sum((ref[...] for ref in weights[1:]), weights[0][...]), keepdims=True)
    weight_out[...] = jnp.broadcast_to(total, weight_out.shape)
    plane = lax.axis_index("member") // lanes
    side = plane // (2 * bit) % 2
    rows = [merged(lanes, owners, plane, bit, keep, got, j) for j in range(keep.shape[0])]
    for j in range(keep_out.shape[0]):
        keep_out[j] = jnp.where(side == 1, rows[2 * j + 1], rows[2 * j])
        give[pl.ds(j * own, own), :] = jnp.where(side == 1, rows[2 * j], rows[2 * j + 1])
    give[pl.ds(keep_out.shape[0] * own, TAIL), :] = weight_rows(total, features)


def encode_kernel(lanes, bit, owners, keep, got, encoder, total, latent, total_out):
    own = latent.shape[0]
    plane = lax.axis_index("member") // lanes
    rows = [got[pl.ds(0, own), :]]
    control = merged(lanes, owners, plane, bit, keep, rows, 0)
    latent[...] = jnp.dot(control, encoder[...], preferred_element_type=F32).astype(BF16)
    total_out[...] = total[...] + weight_from(got[pl.ds(own, TAIL), :])


def prepared(analyses, owners, encoder, area_weight):
    members, regions = lax.axis_size("member"), lax.axis_size("region")
    _, rows, features = analyses.shape
    blocks = owners.shape[0]
    lanes, own = members // blocks, rows // members
    row = jax.ShapeDtypeStruct((own, features), BF16)
    line = jax.ShapeDtypeStruct((1, own), F32)

    def kept(many):
        return jax.ShapeDtypeStruct((many, own, features), BF16)

    *by_lane, own_weight = local_call(
        functools.partial(rows_kernel, lanes),
        [row] * lanes + [line],
        [SMEM] + [HBM] * 2,
        scratch=[pltpu.SemaphoreType.DMA((lanes + 1,))],
        limit=ROWS_LIMIT,
    )(owners, analyses, area_weight[None])
    by_lane = [by_lane[0]] + [swap(by_lane[k], "member", k) for k in range(1, lanes)]
    weight = own_weight
    for bit in bits_of(regions)[:-1]:
        weight = weight + swap(weight, "region", bit)
    across = swap(weight, "region", regions // 2)
    keep, give, weight = local_call(
        functools.partial(blocks_kernel, lanes),
        [kept(blocks // 2)] * 2 + [line],
        [SMEM] + [VMEM] * (lanes + 2),
        limit=8,
    )(owners, *by_lane, weight, across)
    weights = [weight] + [swap(weight, "member", k) for k in range(1, lanes)]
    got = swap(give, "member", lanes)
    small = jax.ShapeDtypeStruct((8, 128), F32)
    keep, give, total = local_call(
        functools.partial(halve_kernel, lanes, 1),
        [kept(1), jax.ShapeDtypeStruct((own + TAIL, features), BF16), small],
        [SMEM] + [VMEM] * (2 + len(weights)),
        limit=8,
    )(owners, keep, got, *weights)
    got = swap(give, "member", 2 * lanes)
    latent, total = local_call(
        functools.partial(encode_kernel, lanes, 2),
        [row, small],
        [SMEM] + [VMEM] * 4,
        flops=2 * own * features * features,
        limit=8,
    )(owners, keep, got, encoder, total)
    return latent, own_weight, total, swap(total, "member", lanes)


def column(row):
    size = row.shape[1]
    first = lax.broadcasted_iota(jnp.int32, (size, size), 0)
    second = lax.broadcasted_iota(jnp.int32, (size, size), 1)
    return jnp.sum(jnp.where(first == second, row, 0.0), axis=1, keepdims=True)


def network(noise, latent, hidden_piece, pieces):
    members, tokens, features = noise.shape
    states = (noise.astype(F32) + latent.astype(F32)[None]).reshape(members * tokens, features)
    mean = jnp.sum(states * states, axis=-1, keepdims=True) * (1.0 / features)
    normed = (states * lax.rsqrt(mean + EPSILON)).astype(BF16)
    total = states
    for piece in range(pieces):
        total = total + hidden_piece(normed, piece)
    return total.astype(BF16)


def score(forecast, targets, scale, members, tokens):
    rows, features = forecast.shape
    gram = lax.dot_general(
        forecast, forecast, (((1,), (1,)), ((), ())), preferred_element_type=F32
    )
    first = lax.broadcasted_iota(jnp.int32, (rows, rows), 0)
    second = lax.broadcasted_iota(jnp.int32, (rows, rows), 1)
    same_row = first == second
    same_token = (first % tokens) == (second % tokens)
    on_diagonal = jnp.where(same_row, gram, 0.0)
    down = jnp.sum(on_diagonal, axis=1, keepdims=True)
    across = jnp.sum(on_diagonal, axis=0, keepdims=True)
    squared = jnp.maximum((down + across - 2.0 * gram) * (1.0 / features), 0.0) + EPSILON
    inverse = lax.rsqrt(squared)
    pairs = jnp.where(same_token, squared * inverse, 0.0)
    coeff = jnp.where(same_token & ~same_row, inverse, 0.0).astype(BF16)
    coeff_sum = jnp.sum(coeff.astype(F32), axis=1, keepdims=True)
    combined = jnp.dot(coeff, forecast, preferred_element_type=F32)
    values = forecast.astype(F32)
    apart = (
        values.reshape(members, tokens, features) - targets.astype(F32)[None]
    )
    squares = jnp.sum(apart * apart, axis=-1, keepdims=True) * (1.0 / features) + EPSILON
    inverse_spread = lax.rsqrt(squares)
    from_others = (coeff_sum * values - combined).reshape(members, tokens, features)
    gradient = scale[None] * (apart * inverse_spread - from_others * (1.0 / members))
    spread = jnp.sum(squares * inverse_spread, axis=0) * (1.0 / members)
    pair_sum = jnp.sum(jnp.sum(pairs, axis=1, keepdims=True).reshape(members, tokens, 1), axis=0)
    energy = scale * (spread - pair_sum * (1.0 / (2.0 * members * members)))
    return gradient, energy


def member_kernel(
    noise,
    latent,
    weight,
    targets_hbm,
    inlet_hbm,
    outlet_hbm,
    gradient_out,
    energy_out,
    targets,
    inlet,
    outlet,
    hidden,
    sems,
):
    members, own, features = noise.shape
    width = inlet.shape[1] // HIDDEN_PIECES
    part = width // INLET_PARTS
    copies = []
    for piece in range(HIDDEN_PIECES):
        for i in range(INLET_PARTS):
            columns = pl.ds(piece * width + i * part, part)
            copies.append((inlet_hbm.at[:, columns], inlet.at[:, columns]))
        rows = pl.ds(piece * width, width)
        copies.append((outlet_hbm.at[rows, :], outlet.at[rows, :]))
    copies = [
        pltpu.make_async_copy(source, target, sems.at[i])
        for i, (source, target) in enumerate(copies)
    ]

    def arrived(i):
        copies[i].wait()
        if i + 2 < len(copies):
            copies[i + 2].start()

    aside = pltpu.make_async_copy(targets_hbm, targets, sems.at[len(copies)])
    for copy in (*copies[:2], aside):
        copy.start()

    def hidden_piece(normed, piece):
        for i in range(INLET_PARTS):
            arrived(piece * (INLET_PARTS + 1) + i)
            first = piece * width + i * part
            hidden[:, i * part : (i + 1) * part] = jax.nn.gelu(
                jnp.dot(normed, inlet[:, first : first + part], preferred_element_type=F32),
                approximate=True,
            ).astype(BF16)
        arrived(piece * (INLET_PARTS + 1) + INLET_PARTS)
        rows = slice(piece * width, (piece + 1) * width)
        return jnp.dot(hidden[...], outlet[rows, :], preferred_element_type=F32)

    forecast = network(noise[...], latent[...], hidden_piece, HIDDEN_PIECES)
    forecast = forecast.reshape(members, own, features)
    aside.wait()
    scales = column(weight[...])
    for first in range(0, own, TOKENS_AT_ONCE):
        here = slice(first, first + TOKENS_AT_ONCE)
        gradient, energy = score(
            forecast[:, here].reshape(members * TOKENS_AT_ONCE, features),
            targets[here, :],
            scales[here, :],
            members,
            TOKENS_AT_ONCE,
        )
        gradient_out[:, here, :] = gradient.astype(BF16)
        energy_out[here, :] = energy


def on_device(
    analyses,
    owners,
    noise,
    targets,
    area_weight,
    enc_weight,
    sample_inlet_matrix,
    sample_outlet_matrix,
):
    members, regions = lax.axis_size("member"), lax.axis_size("region")
    _, region_rows, features = noise.shape
    hidden = sample_inlet_matrix.shape[1]
    own = region_rows // members
    here = transposed(noise.reshape(members, own, features))
    latent, weight, total, across = prepared(analyses, owners, enc_weight, area_weight)
    gradient, energy = local_call(
        member_kernel,
        [
            jax.ShapeDtypeStruct((members, own, features), BF16),
            jax.ShapeDtypeStruct((own, 1), F32),
        ],
        [VMEM] * 3 + [HBM] * 3,
        flops=4 * members * own * features * (hidden + members),
        moved=4 * features * hidden,
        scratch=[
            pltpu.VMEM((own, features), BF16),
            pltpu.VMEM((features, hidden), BF16),
            pltpu.VMEM((hidden, features), BF16),
            pltpu.VMEM((members * own, hidden // HIDDEN_PIECES), BF16),
            pltpu.SemaphoreType.DMA((HIDDEN_PIECES * (INLET_PARTS + 1) + 1,)),
        ],
        limit=NETWORK_LIMIT,
    )(here, latent, weight, targets, sample_inlet_matrix, sample_outlet_matrix)
    gradient, across = lax.optimization_barrier((gradient, across))
    back = transposed(gradient)
    factor = float(region_rows * regions) / (total[0, 0] + across[0, 0])
    member_grad = (back.astype(F32) * factor).astype(BF16).reshape(1, region_rows, features)
    return member_grad, energy[:, 0] * factor


def solution(mesh):
    return jax.shard_map(
        on_device,
        mesh=mesh,
        in_specs=(
            P("member", "region", None),
            P(),
            P("member", "region", None),
            P(("region", "member"), None),
            P(("region", "member")),
            P(),
            P(),
            P(),
        ),
        out_specs=(P("member", "region", None), P(("region", "member"))),
        check_vma=False,
    )
```

```python
import functools

import jax
import jax.numpy as jnp
from jax import lax
from jax.experimental import pallas as pl
from jax.experimental.pallas import tpu as pltpu
from jax.sharding import PartitionSpec as P

EPSILON = 1e-06
TOKENS_AT_ONCE = 16
TAIL = 16
HIDDEN_PIECES = 2
INLET_PARTS = 2
ROWS_LIMIT = 53
NETWORK_LIMIT = 50
BF16 = jnp.bfloat16
F32 = jnp.float32

VMEM = pl.BlockSpec(memory_space=pltpu.VMEM)
SMEM = pl.BlockSpec(memory_space=pltpu.SMEM)
HBM = pl.BlockSpec(memory_space=pltpu.HBM)


def swap(value, axis, bit):
    size = lax.axis_size(axis)
    return lax.ppermute(value, axis, [(i, i ^ bit) for i in range(size)])


def bits_of(size):
    return [1 << i for i in range(size.bit_length() - 1)]


def transposed(value):
    return lax.all_to_all(value, "member", split_axis=0, concat_axis=0, tiled=True)


def local_call(kernel, out_shape, in_specs, flops=0, moved=0, scratch=(), limit=40):
    return pl.pallas_call(
        kernel,
        in_specs=in_specs,
        out_specs=[VMEM] * len(out_shape),
        out_shape=out_shape,
        scratch_shapes=list(scratch),
        compiler_params=pltpu.CompilerParams(vmem_limit_bytes=limit * 2**20),
        cost_estimate=pl.CostEstimate(flops=flops, bytes_accessed=moved, transcendentals=0),
    )


def rows_kernel(lanes, owners, analyses, weight, *refs):
    *outs, weight_out, sems = refs
    own = outs[0].shape[0]
    me = lax.axis_index("member")
    lane = me % lanes
    block = jnp.int32(0)
    for b in range(owners.shape[0]):
        block = jnp.where(owners[b] == me, b, block)
    copies = [
        pltpu.make_async_copy(weight, weight_out, sems.at[lanes]),
    ]
    for k in range(lanes):
        start = pl.multiple_of((block * lanes + (lane ^ k)) * own, own)
        copies.append(
            pltpu.make_async_copy(analyses.at[0, pl.ds(start, own), :], outs[k], sems.at[k])
        )
    for copy in copies:
        copy.start()
    for copy in copies:
        copy.wait()


def blocks_kernel(lanes, owners, *refs):
    held, (weight, across, keep, give, weight_out) = refs[:lanes], refs[lanes:]
    weight_out[...] = weight[...] + across[...]
    me = lax.axis_index("member")
    lane, plane = me % lanes, me // lanes

    def rows_of(block):
        place = (owners[block] % lanes) ^ lane
        rows = held[0][...]
        for k in range(1, lanes):
            rows = jnp.where(place == k, held[k][...], rows)
        return rows

    side = plane % 2
    for j in range(keep.shape[0]):
        keep[j] = rows_of(2 * j + side)
        give[j] = rows_of(2 * j + 1 - side)


def weight_rows(total, features):
    high = total.astype(BF16).astype(F32)
    middle = (total - high).astype(BF16).astype(F32)
    low = total - high - middle
    row = lax.broadcasted_iota(jnp.int32, (TAIL, features), 0)
    picked = jnp.where(row == 0, high, jnp.where(row == 1, middle, jnp.where(row == 2, low, 0.0)))
    return picked.astype(BF16)


def weight_from(rows):
    return jnp.sum(rows[:, 0:128].astype(F32), axis=0, keepdims=True)


def merged(lanes, owners, plane, bit, keep, got, j):
    block = j * (2 * bit) + plane % (2 * bit)
    there = ((owners[block] // lanes) ^ plane) // bit % 2
    return jnp.where(there == 1, got[j], keep[j])


def halve_kernel(lanes, bit, owners, keep, got, *refs):
    *weights, keep_out, give, weight_out = refs
    own, features = keep.shape[1], keep.shape[2]
    total = jnp.sum(sum((ref[...] for ref in weights[1:]), weights[0][...]), keepdims=True)
    weight_out[...] = jnp.broadcast_to(total, weight_out.shape)
    plane = lax.axis_index("member") // lanes
    side = plane // (2 * bit) % 2
    rows = [merged(lanes, owners, plane, bit, keep, got, j) for j in range(keep.shape[0])]
    for j in range(keep_out.shape[0]):
        keep_out[j] = jnp.where(side == 1, rows[2 * j + 1], rows[2 * j])
        give[pl.ds(j * own, own), :] = jnp.where(side == 1, rows[2 * j], rows[2 * j + 1])
    give[pl.ds(keep_out.shape[0] * own, TAIL), :] = weight_rows(total, features)


def encode_kernel(lanes, bit, owners, keep, got, encoder, total, latent, total_out):
    own = latent.shape[0]
    plane = lax.axis_index("member") // lanes
    rows = [got[pl.ds(0, own), :]]
    control = merged(lanes, owners, plane, bit, keep, rows, 0)
    latent[...] = jnp.dot(control, encoder[...], preferred_element_type=F32).astype(BF16)
    total_out[...] = total[...] + weight_from(got[pl.ds(own, TAIL), :])


def prepared(analyses, owners, encoder, area_weight):
    members, regions = lax.axis_size("member"), lax.axis_size("region")
    _, rows, features = analyses.shape
    blocks = owners.shape[0]
    lanes, own = members // blocks, rows // members
    row = jax.ShapeDtypeStruct((own, features), BF16)
    line = jax.ShapeDtypeStruct((1, own), F32)

    def kept(many):
        return jax.ShapeDtypeStruct((many, own, features), BF16)

    *by_lane, own_weight = local_call(
        functools.partial(rows_kernel, lanes),
        [row] * lanes + [line],
        [SMEM] + [HBM] * 2,
        scratch=[pltpu.SemaphoreType.DMA((lanes + 1,))],
        limit=ROWS_LIMIT,
    )(owners, analyses, area_weight[None])
    by_lane = [by_lane[0]] + [swap(by_lane[k], "member", k) for k in range(1, lanes)]
    weight = own_weight
    for bit in bits_of(regions)[:-1]:
        weight = weight + swap(weight, "region", bit)
    across = swap(weight, "region", regions // 2)
    keep, give, weight = local_call(
        functools.partial(blocks_kernel, lanes),
        [kept(blocks // 2)] * 2 + [line],
        [SMEM] + [VMEM] * (lanes + 2),
        limit=8,
    )(owners, *by_lane, weight, across)
    weights = [weight] + [swap(weight, "member", k) for k in range(1, lanes)]
    got = swap(give, "member", lanes)
    small = jax.ShapeDtypeStruct((8, 128), F32)
    keep, give, total = local_call(
        functools.partial(halve_kernel, lanes, 1),
        [kept(1), jax.ShapeDtypeStruct((own + TAIL, features), BF16), small],
        [SMEM] + [VMEM] * (2 + len(weights)),
        limit=8,
    )(owners, keep, got, *weights)
    got = swap(give, "member", 2 * lanes)
    latent, total = local_call(
        functools.partial(encode_kernel, lanes, 2),
        [row, small],
        [SMEM] + [VMEM] * 4,
        flops=2 * own * features * features,
        limit=8,
    )(owners, keep, got, encoder, total)
    return latent, own_weight, total


def column(row):
    size = row.shape[1]
    first = lax.broadcasted_iota(jnp.int32, (size, size), 0)
    second = lax.broadcasted_iota(jnp.int32, (size, size), 1)
    return jnp.sum(jnp.where(first == second, row, 0.0), axis=1, keepdims=True)


def network(noise, latent, hidden_piece, pieces):
    members, tokens, features = noise.shape
    states = (noise.astype(F32) + latent.astype(F32)[None]).reshape(members * tokens, features)
    mean = jnp.sum(states * states, axis=-1, keepdims=True) * (1.0 / features)
    normed = (states * lax.rsqrt(mean + EPSILON)).astype(BF16)
    total = states
    for piece in range(pieces):
        total = total + hidden_piece(normed, piece)
    return total.astype(BF16)


def score(forecast, targets, scale, members, tokens):
    rows, features = forecast.shape
    gram = lax.dot_general(
        forecast, forecast, (((1,), (1,)), ((), ())), preferred_element_type=F32
    )
    first = lax.broadcasted_iota(jnp.int32, (rows, rows), 0)
    second = lax.broadcasted_iota(jnp.int32, (rows, rows), 1)
    same_row = first == second
    same_token = (first % tokens) == (second % tokens)
    on_diagonal = jnp.where(same_row, gram, 0.0)
    down = jnp.sum(on_diagonal, axis=1, keepdims=True)
    across = jnp.sum(on_diagonal, axis=0, keepdims=True)
    squared = jnp.maximum((down + across - 2.0 * gram) * (1.0 / features), 0.0) + EPSILON
    inverse = lax.rsqrt(squared)
    pairs = jnp.where(same_token, squared * inverse, 0.0)
    coeff = jnp.where(same_token & ~same_row, inverse, 0.0).astype(BF16)
    coeff_sum = jnp.sum(coeff.astype(F32), axis=1, keepdims=True)
    combined = jnp.dot(coeff, forecast, preferred_element_type=F32)
    values = forecast.astype(F32)
    apart = (
        values.reshape(members, tokens, features) - targets.astype(F32)[None]
    )
    squares = jnp.sum(apart * apart, axis=-1, keepdims=True) * (1.0 / features) + EPSILON
    inverse_spread = lax.rsqrt(squares)
    from_others = (coeff_sum * values - combined).reshape(members, tokens, features)
    gradient = scale[None] * (apart * inverse_spread - from_others * (1.0 / members))
    spread = jnp.sum(squares * inverse_spread, axis=0) * (1.0 / members)
    pair_sum = jnp.sum(jnp.sum(pairs, axis=1, keepdims=True).reshape(members, tokens, 1), axis=0)
    energy = scale * (spread - pair_sum * (1.0 / (2.0 * members * members)))
    return gradient, energy


def member_kernel(
    noise,
    latent,
    weight,
    targets_hbm,
    inlet_hbm,
    outlet_hbm,
    gradient_out,
    energy_out,
    targets,
    inlet,
    outlet,
    hidden,
    sems,
):
    members, own, features = noise.shape
    width = inlet.shape[1] // HIDDEN_PIECES
    part = width // INLET_PARTS
    copies = []
    for piece in range(HIDDEN_PIECES):
        for i in range(INLET_PARTS):
            columns = pl.ds(piece * width + i * part, part)
            copies.append((inlet_hbm.at[:, columns], inlet.at[:, columns]))
        rows = pl.ds(piece * width, width)
        copies.append((outlet_hbm.at[rows, :], outlet.at[rows, :]))
    copies = [
        pltpu.make_async_copy(source, target, sems.at[i])
        for i, (source, target) in enumerate(copies)
    ]

    def arrived(i):
        copies[i].wait()
        if i + 2 < len(copies):
            copies[i + 2].start()

    aside = pltpu.make_async_copy(targets_hbm, targets, sems.at[len(copies)])
    for copy in (*copies[:2], aside):
        copy.start()

    def hidden_piece(normed, piece):
        for i in range(INLET_PARTS):
            arrived(piece * (INLET_PARTS + 1) + i)
            first = piece * width + i * part
            hidden[:, i * part : (i + 1) * part] = jax.nn.gelu(
                jnp.dot(normed, inlet[:, first : first + part], preferred_element_type=F32),
                approximate=True,
            ).astype(BF16)
        arrived(piece * (INLET_PARTS + 1) + INLET_PARTS)
        rows = slice(piece * width, (piece + 1) * width)
        return jnp.dot(hidden[...], outlet[rows, :], preferred_element_type=F32)

    forecast = network(noise[...], latent[...], hidden_piece, HIDDEN_PIECES)
    forecast = forecast.reshape(members, own, features)
    aside.wait()
    scales = column(weight[...])
    for first in range(0, own, TOKENS_AT_ONCE):
        here = slice(first, first + TOKENS_AT_ONCE)
        gradient, energy = score(
            forecast[:, here].reshape(members * TOKENS_AT_ONCE, features),
            targets[here, :],
            scales[here, :],
            members,
            TOKENS_AT_ONCE,
        )
        gradient_out[:, here, :] = gradient.astype(BF16)
        energy_out[here, :] = energy


def on_device(
    analyses,
    owners,
    noise,
    targets,
    area_weight,
    enc_weight,
    sample_inlet_matrix,
    sample_outlet_matrix,
):
    members, regions = lax.axis_size("member"), lax.axis_size("region")
    _, region_rows, features = noise.shape
    hidden = sample_inlet_matrix.shape[1]
    own = region_rows // members
    here = transposed(noise.reshape(members, own, features))
    latent, weight, total = prepared(analyses, owners, enc_weight, area_weight)
    gradient, energy = local_call(
        member_kernel,
        [
            jax.ShapeDtypeStruct((members, own, features), BF16),
            jax.ShapeDtypeStruct((own, 1), F32),
        ],
        [VMEM] * 3 + [HBM] * 3,
        flops=4 * members * own * features * (hidden + members),
        moved=4 * features * hidden,
        scratch=[
            pltpu.VMEM((own, features), BF16),
            pltpu.VMEM((features, hidden), BF16),
            pltpu.VMEM((hidden, features), BF16),
            pltpu.VMEM((members * own, hidden // HIDDEN_PIECES), BF16),
            pltpu.SemaphoreType.DMA((HIDDEN_PIECES * (INLET_PARTS + 1) + 1,)),
        ],
        limit=NETWORK_LIMIT,
    )(here, latent, weight, targets, sample_inlet_matrix, sample_outlet_matrix)
    gradient, total = lax.optimization_barrier((gradient, total))
    back = transposed(gradient)
    across = swap(total, "member", members // owners.shape[0])
    factor = float(region_rows * regions) / (total[0, 0] + across[0, 0])
    member_grad = (back.astype(F32) * factor).astype(BF16).reshape(1, region_rows, features)
    return member_grad, energy[:, 0] * factor


def solution(mesh):
    return jax.shard_map(
        on_device,
        mesh=mesh,
        in_specs=(
            P("member", "region", None),
            P(),
            P("member", "region", None),
            P(("region", "member"), None),
            P(("region", "member")),
            P(),
            P(),
            P(),
        ),
        out_specs=(P("member", "region", None), P(("region", "member"))),
        check_vma=False,
    )
```

```python
import functools

import jax
import jax.numpy as jnp
from jax import lax
from jax.experimental import pallas as pl
from jax.experimental.pallas import tpu as pltpu
from jax.sharding import PartitionSpec as P

EPSILON = 1e-06
TOKENS_AT_ONCE = 16
TAIL = 16
HIDDEN_PIECES = 2
ROWS_LIMIT = 53
NETWORK_LIMIT = 46
FETCH_LIMIT = 46
BF16 = jnp.bfloat16
F32 = jnp.float32

VMEM = pl.BlockSpec(memory_space=pltpu.VMEM)
SMEM = pl.BlockSpec(memory_space=pltpu.SMEM)
HBM = pl.BlockSpec(memory_space=pltpu.HBM)


def swap(value, axis, bit):
    size = lax.axis_size(axis)
    return lax.ppermute(value, axis, [(i, i ^ bit) for i in range(size)])


def bits_of(size):
    return [1 << i for i in range(size.bit_length() - 1)]


def transposed(value):
    return lax.all_to_all(value, "member", split_axis=0, concat_axis=0, tiled=True)


def local_call(kernel, out_shape, in_specs, flops=0, moved=0, scratch=(), limit=40):
    return pl.pallas_call(
        kernel,
        in_specs=in_specs,
        out_specs=[VMEM] * len(out_shape),
        out_shape=out_shape,
        scratch_shapes=list(scratch),
        compiler_params=pltpu.CompilerParams(vmem_limit_bytes=limit * 2**20),
        cost_estimate=pl.CostEstimate(flops=flops, bytes_accessed=moved, transcendentals=0),
    )


def rows_kernel(lanes, owners, analyses, weight, *refs):
    *outs, weight_out, sems = refs
    own = outs[0].shape[0]
    me = lax.axis_index("member")
    lane = me % lanes
    block = jnp.int32(0)
    for b in range(owners.shape[0]):
        block = jnp.where(owners[b] == me, b, block)
    copies = [
        pltpu.make_async_copy(weight, weight_out, sems.at[lanes]),
    ]
    for k in range(lanes):
        start = pl.multiple_of((block * lanes + (lane ^ k)) * own, own)
        copies.append(
            pltpu.make_async_copy(analyses.at[0, pl.ds(start, own), :], outs[k], sems.at[k])
        )
    for copy in copies:
        copy.start()
    for copy in copies:
        copy.wait()


def blocks_kernel(lanes, owners, *refs):
    held, (weight, across, keep, give, weight_out) = refs[:lanes], refs[lanes:]
    weight_out[...] = weight[...] + across[...]
    me = lax.axis_index("member")
    lane, plane = me % lanes, me // lanes

    def rows_of(block):
        place = (owners[block] % lanes) ^ lane
        rows = held[0][...]
        for k in range(1, lanes):
            rows = jnp.where(place == k, held[k][...], rows)
        return rows

    side = plane % 2
    for j in range(keep.shape[0]):
        keep[j] = rows_of(2 * j + side)
        give[j] = rows_of(2 * j + 1 - side)


def weight_rows(total, features):
    high = total.astype(BF16).astype(F32)
    middle = (total - high).astype(BF16).astype(F32)
    low = total - high - middle
    row = lax.broadcasted_iota(jnp.int32, (TAIL, features), 0)
    picked = jnp.where(row == 0, high, jnp.where(row == 1, middle, jnp.where(row == 2, low, 0.0)))
    return picked.astype(BF16)


def weight_from(rows):
    return jnp.sum(rows[:, 0:128].astype(F32), axis=0, keepdims=True)


def merged(lanes, owners, plane, bit, keep, got, j):
    block = j * (2 * bit) + plane % (2 * bit)
    there = ((owners[block] // lanes) ^ plane) // bit % 2
    return jnp.where(there == 1, got[j], keep[j])


def halve_kernel(lanes, bit, owners, keep, got, *refs):
    *weights, keep_out, give, weight_out = refs
    own, features = keep.shape[1], keep.shape[2]
    total = jnp.sum(sum((ref[...] for ref in weights[1:]), weights[0][...]), keepdims=True)
    weight_out[...] = jnp.broadcast_to(total, weight_out.shape)
    plane = lax.axis_index("member") // lanes
    side = plane // (2 * bit) % 2
    rows = [merged(lanes, owners, plane, bit, keep, got, j) for j in range(keep.shape[0])]
    for j in range(keep_out.shape[0]):
        keep_out[j] = jnp.where(side == 1, rows[2 * j + 1], rows[2 * j])
        give[pl.ds(j * own, own), :] = jnp.where(side == 1, rows[2 * j], rows[2 * j + 1])
    give[pl.ds(keep_out.shape[0] * own, TAIL), :] = weight_rows(total, features)


def fetch_kernel(matrix, after, near, sem):
    copy = pltpu.make_async_copy(matrix, near, sem)
    copy.start()
    copy.wait()


def encode_kernel(lanes, bit, owners, keep, got, encoder, total, latent, total_out):
    own = latent.shape[0]
    plane = lax.axis_index("member") // lanes
    rows = [got[pl.ds(0, own), :]]
    control = merged(lanes, owners, plane, bit, keep, rows, 0)
    latent[...] = jnp.dot(control, encoder[...], preferred_element_type=F32).astype(BF16)
    total_out[...] = total[...] + weight_from(got[pl.ds(own, TAIL), :])


def prepared(analyses, owners, encoder, area_weight, matrix, after):
    members, regions = lax.axis_size("member"), lax.axis_size("region")
    _, rows, features = analyses.shape
    blocks = owners.shape[0]
    lanes, own = members // blocks, rows // members
    row = jax.ShapeDtypeStruct((own, features), BF16)
    line = jax.ShapeDtypeStruct((1, own), F32)

    def kept(many):
        return jax.ShapeDtypeStruct((many, own, features), BF16)

    *by_lane, own_weight = local_call(
        functools.partial(rows_kernel, lanes),
        [row] * lanes + [line],
        [SMEM] + [HBM] * 2,
        scratch=[pltpu.SemaphoreType.DMA((lanes + 1,))],
        limit=ROWS_LIMIT,
    )(owners, analyses, area_weight[None])
    by_lane = [by_lane[0]] + [swap(by_lane[k], "member", k) for k in range(1, lanes)]
    weight = own_weight
    for bit in bits_of(regions)[:-1]:
        weight = weight + swap(weight, "region", bit)
    across = swap(weight, "region", regions // 2)
    keep, give, weight = local_call(
        functools.partial(blocks_kernel, lanes),
        [kept(blocks // 2)] * 2 + [line],
        [SMEM] + [VMEM] * (lanes + 2),
        limit=8,
    )(owners, *by_lane, weight, across)
    weights = [weight] + [swap(weight, "member", k) for k in range(1, lanes)]
    got = swap(give, "member", lanes)
    small = jax.ShapeDtypeStruct((8, 128), F32)
    keep, give, total = local_call(
        functools.partial(halve_kernel, lanes, 1),
        [kept(1), jax.ShapeDtypeStruct((own + TAIL, features), BF16), small],
        [SMEM] + [VMEM] * (2 + len(weights)),
        limit=8,
    )(owners, keep, got, *weights)
    got = swap(give, "member", 2 * lanes)
    (near,) = local_call(
        fetch_kernel,
        [jax.ShapeDtypeStruct(matrix.shape, BF16)],
        [HBM, VMEM],
        moved=2 * matrix.size,
        scratch=[pltpu.SemaphoreType.DMA],
        limit=FETCH_LIMIT,
    )(matrix, after)
    got, near = lax.optimization_barrier((got, near))
    latent, total = local_call(
        functools.partial(encode_kernel, lanes, 2),
        [row, small],
        [SMEM] + [VMEM] * 4,
        flops=2 * own * features * features,
        limit=8,
    )(owners, keep, got, encoder, total)
    return latent, own_weight, total, near


def column(row):
    size = row.shape[1]
    first = lax.broadcasted_iota(jnp.int32, (size, size), 0)
    second = lax.broadcasted_iota(jnp.int32, (size, size), 1)
    return jnp.sum(jnp.where(first == second, row, 0.0), axis=1, keepdims=True)


def network(noise, latent, hidden_piece, pieces):
    members, tokens, features = noise.shape
    states = (noise.astype(F32) + latent.astype(F32)[None]).reshape(members * tokens, features)
    mean = jnp.sum(states * states, axis=-1, keepdims=True) * (1.0 / features)
    normed = (states * lax.rsqrt(mean + EPSILON)).astype(BF16)
    total = states
    for piece in range(pieces):
        total = total + hidden_piece(normed, piece)
    return total.astype(BF16)


def score(forecast, targets, scale, members, tokens):
    rows, features = forecast.shape
    gram = lax.dot_general(
        forecast, forecast, (((1,), (1,)), ((), ())), preferred_element_type=F32
    )
    first = lax.broadcasted_iota(jnp.int32, (rows, rows), 0)
    second = lax.broadcasted_iota(jnp.int32, (rows, rows), 1)
    same_row = first == second
    same_token = (first % tokens) == (second % tokens)
    on_diagonal = jnp.where(same_row, gram, 0.0)
    down = jnp.sum(on_diagonal, axis=1, keepdims=True)
    across = jnp.sum(on_diagonal, axis=0, keepdims=True)
    squared = jnp.maximum((down + across - 2.0 * gram) * (1.0 / features), 0.0) + EPSILON
    inverse = lax.rsqrt(squared)
    pairs = jnp.where(same_token, squared * inverse, 0.0)
    coeff = jnp.where(same_token & ~same_row, inverse, 0.0).astype(BF16)
    coeff_sum = jnp.sum(coeff.astype(F32), axis=1, keepdims=True)
    combined = jnp.dot(coeff, forecast, preferred_element_type=F32)
    values = forecast.astype(F32)
    apart = (
        values.reshape(members, tokens, features) - targets.astype(F32)[None]
    )
    squares = jnp.sum(apart * apart, axis=-1, keepdims=True) * (1.0 / features) + EPSILON
    inverse_spread = lax.rsqrt(squares)
    from_others = (coeff_sum * values - combined).reshape(members, tokens, features)
    gradient = scale[None] * (apart * inverse_spread - from_others * (1.0 / members))
    spread = jnp.sum(squares * inverse_spread, axis=0) * (1.0 / members)
    pair_sum = jnp.sum(jnp.sum(pairs, axis=1, keepdims=True).reshape(members, tokens, 1), axis=0)
    energy = scale * (spread - pair_sum * (1.0 / (2.0 * members * members)))
    return gradient, energy


def member_kernel(
    noise,
    latent,
    weight,
    inlet,
    targets_hbm,
    outlet_hbm,
    gradient_out,
    energy_out,
    targets,
    outlet,
    hidden,
    sems,
):
    members, own, features = noise.shape
    width = inlet.shape[1] // HIDDEN_PIECES
    copies = [pltpu.make_async_copy(targets_hbm, targets, sems.at[HIDDEN_PIECES])]
    for piece in range(HIDDEN_PIECES):
        rows = pl.ds(piece * width, width)
        copies.append(
            pltpu.make_async_copy(outlet_hbm.at[rows, :], outlet.at[rows, :], sems.at[piece])
        )
    for copy in copies:
        copy.start()

    def hidden_piece(normed, piece):
        rows = slice(piece * width, (piece + 1) * width)
        hidden[...] = jax.nn.gelu(
            jnp.dot(normed, inlet[:, rows], preferred_element_type=F32), approximate=True
        ).astype(BF16)
        copies[piece + 1].wait()
        return jnp.dot(hidden[...], outlet[rows, :], preferred_element_type=F32)

    forecast = network(noise[...], latent[...], hidden_piece, HIDDEN_PIECES)
    forecast = forecast.reshape(members, own, features)
    copies[0].wait()
    scales = column(weight[...])
    for first in range(0, own, TOKENS_AT_ONCE):
        here = slice(first, first + TOKENS_AT_ONCE)
        gradient, energy = score(
            forecast[:, here].reshape(members * TOKENS_AT_ONCE, features),
            targets[here, :],
            scales[here, :],
            members,
            TOKENS_AT_ONCE,
        )
        gradient_out[:, here, :] = gradient.astype(BF16)
        energy_out[here, :] = energy


def on_device(
    analyses,
    owners,
    noise,
    targets,
    area_weight,
    enc_weight,
    sample_inlet_matrix,
    sample_outlet_matrix,
):
    members, regions = lax.axis_size("member"), lax.axis_size("region")
    _, region_rows, features = noise.shape
    hidden = sample_inlet_matrix.shape[1]
    own = region_rows // members
    here = transposed(noise.reshape(members, own, features))
    latent, weight, total, inlet = prepared(
        analyses, owners, enc_weight, area_weight, sample_inlet_matrix, here
    )
    gradient, energy = local_call(
        member_kernel,
        [
            jax.ShapeDtypeStruct((members, own, features), BF16),
            jax.ShapeDtypeStruct((own, 1), F32),
        ],
        [VMEM] * 4 + [HBM] * 2,
        flops=4 * members * own * features * (hidden + members),
        moved=4 * features * hidden,
        scratch=[
            pltpu.VMEM((own, features), BF16),
            pltpu.VMEM((hidden, features), BF16),
            pltpu.VMEM((members * own, hidden // HIDDEN_PIECES), BF16),
            pltpu.SemaphoreType.DMA((HIDDEN_PIECES + 1,)),
        ],
        limit=NETWORK_LIMIT,
    )(here, latent, weight, inlet, targets, sample_outlet_matrix)
    gradient, total = lax.optimization_barrier((gradient, total))
    back = transposed(gradient)
    across = swap(total, "member", members // owners.shape[0])
    factor = float(region_rows * regions) / (total[0, 0] + across[0, 0])
    member_grad = (back.astype(F32) * factor).astype(BF16).reshape(1, region_rows, features)
    return member_grad, energy[:, 0] * factor


def solution(mesh):
    return jax.shard_map(
        on_device,
        mesh=mesh,
        in_specs=(
            P("member", "region", None),
            P(),
            P("member", "region", None),
            P(("region", "member"), None),
            P(("region", "member")),
            P(),
            P(),
            P(),
        ),
        out_specs=(P("member", "region", None), P(("region", "member"))),
        check_vma=False,
    )
```

```python
import functools

import jax
import jax.numpy as jnp
from jax import lax
from jax.experimental import pallas as pl
from jax.experimental.pallas import tpu as pltpu
from jax.sharding import PartitionSpec as P

EPSILON = 1e-06
TOKENS_AT_ONCE = 16
HIDDEN_PIECES = 2
ROWS_LIMIT = 53
NETWORK_LIMIT = 46
FETCH_LIMIT = 46
BF16 = jnp.bfloat16
F32 = jnp.float32

VMEM = pl.BlockSpec(memory_space=pltpu.VMEM)
SMEM = pl.BlockSpec(memory_space=pltpu.SMEM)
HBM = pl.BlockSpec(memory_space=pltpu.HBM)


def swap(value, axis, bit):
    size = lax.axis_size(axis)
    return lax.ppermute(value, axis, [(i, i ^ bit) for i in range(size)])


def bits_of(size):
    return [1 << i for i in range(size.bit_length() - 1)]


def transposed(value):
    return lax.all_to_all(value, "member", split_axis=0, concat_axis=0, tiled=True)


def local_call(kernel, out_shape, in_specs, flops=0, moved=0, scratch=(), limit=40):
    return pl.pallas_call(
        kernel,
        in_specs=in_specs,
        out_specs=[VMEM] * len(out_shape),
        out_shape=out_shape,
        scratch_shapes=list(scratch),
        compiler_params=pltpu.CompilerParams(vmem_limit_bytes=limit * 2**20),
        cost_estimate=pl.CostEstimate(flops=flops, bytes_accessed=moved, transcendentals=0),
    )


def rows_kernel(lanes, owners, analyses, weight, *refs):
    *outs, weight_out, sems = refs
    own = outs[0].shape[0]
    me = lax.axis_index("member")
    lane = me % lanes
    block = jnp.int32(0)
    for b in range(owners.shape[0]):
        block = jnp.where(owners[b] == me, b, block)
    copies = [
        pltpu.make_async_copy(weight, weight_out, sems.at[lanes]),
    ]
    for k in range(lanes):
        start = pl.multiple_of((block * lanes + (lane ^ k)) * own, own)
        copies.append(
            pltpu.make_async_copy(analyses.at[0, pl.ds(start, own), :], outs[k], sems.at[k])
        )
    for copy in copies:
        copy.start()
    for copy in copies:
        copy.wait()


def planes_kernel(lanes, owners, *refs):
    held, (weight, across, *outs, weight_out) = refs[:lanes], refs[lanes:]
    weight_out[...] = weight[...] + across[...]
    me = lax.axis_index("member")
    lane, plane = me % lanes, me // lanes
    for j, out in enumerate(outs):
        place = (owners[plane ^ j] % lanes) ^ lane
        rows = held[0][...]
        for k in range(1, lanes):
            rows = jnp.where(place == k, held[k][...], rows)
        out[...] = rows


def fetch_kernel(matrix, after, near, sem):
    copy = pltpu.make_async_copy(matrix, near, sem)
    copy.start()
    copy.wait()


def encode_kernel(lanes, blocks, owners, encoder, *refs):
    held, (*weights, latent, total_out) = refs[:blocks], refs[blocks:]
    plane = lax.axis_index("member") // lanes
    place = (owners[plane] // lanes) ^ plane
    control = held[0][...]
    for k in range(1, blocks):
        control = jnp.where(place == k, held[k][...], control)
    latent[...] = jnp.dot(control, encoder[...], preferred_element_type=F32).astype(BF16)
    total = jnp.sum(sum((ref[...] for ref in weights[1:]), weights[0][...]), keepdims=True)
    total_out[...] = jnp.broadcast_to(total, total_out.shape)


def prepared(analyses, owners, encoder, area_weight, matrix, after):
    members, regions = lax.axis_size("member"), lax.axis_size("region")
    _, rows, features = analyses.shape
    blocks = owners.shape[0]
    lanes, own = members // blocks, rows // members
    row = jax.ShapeDtypeStruct((own, features), BF16)
    line = jax.ShapeDtypeStruct((1, own), F32)

    *by_lane, own_weight = local_call(
        functools.partial(rows_kernel, lanes),
        [row] * lanes + [line],
        [SMEM] + [HBM] * 2,
        scratch=[pltpu.SemaphoreType.DMA((lanes + 1,))],
        limit=ROWS_LIMIT,
    )(owners, analyses, area_weight[None])
    by_lane = [by_lane[0]] + [swap(by_lane[k], "member", k) for k in range(1, lanes)]
    weight = own_weight
    for bit in bits_of(regions)[:-1]:
        weight = weight + swap(weight, "region", bit)
    across = swap(weight, "region", regions // 2)
    *by_plane, weight = local_call(
        functools.partial(planes_kernel, lanes),
        [row] * blocks + [line],
        [SMEM] + [VMEM] * (lanes + 2),
        limit=8,
    )(owners, *by_lane, weight, across)
    by_plane = [by_plane[0]] + [
        swap(by_plane[k], "member", k * lanes) for k in range(1, blocks)
    ]
    weights = [weight] + [swap(weight, "member", k) for k in range(1, lanes)]
    (near,) = local_call(
        fetch_kernel,
        [jax.ShapeDtypeStruct(matrix.shape, BF16)],
        [HBM, VMEM],
        moved=2 * matrix.size,
        scratch=[pltpu.SemaphoreType.DMA],
        limit=FETCH_LIMIT,
    )(matrix, after)
    near, *by_plane = lax.optimization_barrier((near, *by_plane))
    latent, total = local_call(
        functools.partial(encode_kernel, lanes, blocks),
        [row, jax.ShapeDtypeStruct((8, 128), F32)],
        [SMEM] + [VMEM] * (1 + blocks + lanes),
        flops=2 * own * features * features,
        limit=8,
    )(owners, encoder, *by_plane, *weights)
    return latent, own_weight, total, near


def column(row):
    size = row.shape[1]
    first = lax.broadcasted_iota(jnp.int32, (size, size), 0)
    second = lax.broadcasted_iota(jnp.int32, (size, size), 1)
    return jnp.sum(jnp.where(first == second, row, 0.0), axis=1, keepdims=True)


def network(noise, latent, hidden_piece, pieces):
    members, tokens, features = noise.shape
    states = (noise.astype(F32) + latent.astype(F32)[None]).reshape(members * tokens, features)
    mean = jnp.sum(states * states, axis=-1, keepdims=True) * (1.0 / features)
    normed = (states * lax.rsqrt(mean + EPSILON)).astype(BF16)
    total = states
    for piece in range(pieces):
        total = total + hidden_piece(normed, piece)
    return total.astype(BF16)


def score(forecast, targets, scale, members, tokens):
    rows, features = forecast.shape
    gram = lax.dot_general(
        forecast, forecast, (((1,), (1,)), ((), ())), preferred_element_type=F32
    )
    first = lax.broadcasted_iota(jnp.int32, (rows, rows), 0)
    second = lax.broadcasted_iota(jnp.int32, (rows, rows), 1)
    same_row = first == second
    same_token = (first % tokens) == (second % tokens)
    on_diagonal = jnp.where(same_row, gram, 0.0)
    down = jnp.sum(on_diagonal, axis=1, keepdims=True)
    across = jnp.sum(on_diagonal, axis=0, keepdims=True)
    squared = jnp.maximum((down + across - 2.0 * gram) * (1.0 / features), 0.0) + EPSILON
    inverse = lax.rsqrt(squared)
    pairs = jnp.where(same_token, squared * inverse, 0.0)
    coeff = jnp.where(same_token & ~same_row, inverse, 0.0).astype(BF16)
    coeff_sum = jnp.sum(coeff.astype(F32), axis=1, keepdims=True)
    combined = jnp.dot(coeff, forecast, preferred_element_type=F32)
    values = forecast.astype(F32)
    apart = (
        values.reshape(members, tokens, features) - targets.astype(F32)[None]
    )
    squares = jnp.sum(apart * apart, axis=-1, keepdims=True) * (1.0 / features) + EPSILON
    inverse_spread = lax.rsqrt(squares)
    from_others = (coeff_sum * values - combined).reshape(members, tokens, features)
    gradient = scale[None] * (apart * inverse_spread - from_others * (1.0 / members))
    spread = jnp.sum(squares * inverse_spread, axis=0) * (1.0 / members)
    pair_sum = jnp.sum(jnp.sum(pairs, axis=1, keepdims=True).reshape(members, tokens, 1), axis=0)
    energy = scale * (spread - pair_sum * (1.0 / (2.0 * members * members)))
    return gradient, energy


def member_kernel(
    noise,
    latent,
    weight,
    inlet,
    targets_hbm,
    outlet_hbm,
    gradient_out,
    energy_out,
    targets,
    outlet,
    hidden,
    sems,
):
    members, own, features = noise.shape
    width = inlet.shape[1] // HIDDEN_PIECES
    copies = [pltpu.make_async_copy(targets_hbm, targets, sems.at[HIDDEN_PIECES])]
    for piece in range(HIDDEN_PIECES):
        rows = pl.ds(piece * width, width)
        copies.append(
            pltpu.make_async_copy(outlet_hbm.at[rows, :], outlet.at[rows, :], sems.at[piece])
        )
    for copy in copies:
        copy.start()

    def hidden_piece(normed, piece):
        rows = slice(piece * width, (piece + 1) * width)
        hidden[...] = jax.nn.gelu(
            jnp.dot(normed, inlet[:, rows], preferred_element_type=F32), approximate=True
        ).astype(BF16)
        copies[piece + 1].wait()
        return jnp.dot(hidden[...], outlet[rows, :], preferred_element_type=F32)

    forecast = network(noise[...], latent[...], hidden_piece, HIDDEN_PIECES)
    forecast = forecast.reshape(members, own, features)
    copies[0].wait()
    scales = column(weight[...])
    for first in range(0, own, TOKENS_AT_ONCE):
        here = slice(first, first + TOKENS_AT_ONCE)
        gradient, energy = score(
            forecast[:, here].reshape(members * TOKENS_AT_ONCE, features),
            targets[here, :],
            scales[here, :],
            members,
            TOKENS_AT_ONCE,
        )
        gradient_out[:, here, :] = gradient.astype(BF16)
        energy_out[here, :] = energy


def on_device(
    analyses,
    owners,
    noise,
    targets,
    area_weight,
    enc_weight,
    sample_inlet_matrix,
    sample_outlet_matrix,
):
    members, regions = lax.axis_size("member"), lax.axis_size("region")
    _, region_rows, features = noise.shape
    hidden = sample_inlet_matrix.shape[1]
    own = region_rows // members
    here = transposed(noise.reshape(members, own, features))
    latent, weight, total, inlet = prepared(
        analyses, owners, enc_weight, area_weight, sample_inlet_matrix, here
    )
    gradient, energy = local_call(
        member_kernel,
        [
            jax.ShapeDtypeStruct((members, own, features), BF16),
            jax.ShapeDtypeStruct((own, 1), F32),
        ],
        [VMEM] * 4 + [HBM] * 2,
        flops=4 * members * own * features * (hidden + members),
        moved=4 * features * hidden,
        scratch=[
            pltpu.VMEM((own, features), BF16),
            pltpu.VMEM((hidden, features), BF16),
            pltpu.VMEM((members * own, hidden // HIDDEN_PIECES), BF16),
            pltpu.SemaphoreType.DMA((HIDDEN_PIECES + 1,)),
        ],
        limit=NETWORK_LIMIT,
    )(here, latent, weight, inlet, targets, sample_outlet_matrix)
    gradient, total = lax.optimization_barrier((gradient, total))
    back = transposed(gradient)
    lanes = members // owners.shape[0]
    total = sum(
        (swap(total, "member", k * lanes) for k in range(1, owners.shape[0])), total
    )
    factor = float(region_rows * regions) / total[0, 0]
    member_grad = (back.astype(F32) * factor).astype(BF16).reshape(1, region_rows, features)
    return member_grad, energy[:, 0] * factor


def solution(mesh):
    return jax.shard_map(
        on_device,
        mesh=mesh,
        in_specs=(
            P("member", "region", None),
            P(),
            P("member", "region", None),
            P(("region", "member"), None),
            P(("region", "member")),
            P(),
            P(),
            P(),
        ),
        out_specs=(P("member", "region", None), P(("region", "member"))),
        check_vma=False,
    )
```

```python
import functools

import jax
import jax.numpy as jnp
from jax import lax
from jax.experimental import pallas as pl
from jax.experimental.pallas import tpu as pltpu
from jax.sharding import PartitionSpec as P

EPSILON = 1e-06
TOKENS_AT_ONCE = 16
TAIL = 16
HIDDEN_PIECES = 2
ROWS_LIMIT = 53
NETWORK_LIMIT = 42
FETCH_LIMIT = 44
BF16 = jnp.bfloat16
F32 = jnp.float32

VMEM = pl.BlockSpec(memory_space=pltpu.VMEM)
SMEM = pl.BlockSpec(memory_space=pltpu.SMEM)
HBM = pl.BlockSpec(memory_space=pltpu.HBM)


def swap(value, axis, bit):
    size = lax.axis_size(axis)
    return lax.ppermute(value, axis, [(i, i ^ bit) for i in range(size)])


def bits_of(size):
    return [1 << i for i in range(size.bit_length() - 1)]


def transposed(value):
    return lax.all_to_all(value, "member", split_axis=0, concat_axis=0, tiled=True)


def local_call(
    kernel, out_shape, in_specs, flops=0, moved=0, scratch=(), limit=40, out_specs=None
):
    return pl.pallas_call(
        kernel,
        in_specs=in_specs,
        out_specs=out_specs or [VMEM] * len(out_shape),
        out_shape=out_shape,
        scratch_shapes=list(scratch),
        compiler_params=pltpu.CompilerParams(vmem_limit_bytes=limit * 2**20),
        cost_estimate=pl.CostEstimate(flops=flops, bytes_accessed=moved, transcendentals=0),
    )


def rows_kernel(lanes, owners, analyses, weight, *refs):
    *outs, weight_out, sems = refs
    own = outs[0].shape[0]
    me = lax.axis_index("member")
    lane = me % lanes
    block = jnp.int32(0)
    for b in range(owners.shape[0]):
        block = jnp.where(owners[b] == me, b, block)
    copies = [
        pltpu.make_async_copy(weight, weight_out, sems.at[lanes]),
    ]
    for k in range(lanes):
        start = pl.multiple_of((block * lanes + (lane ^ k)) * own, own)
        copies.append(
            pltpu.make_async_copy(analyses.at[0, pl.ds(start, own), :], outs[k], sems.at[k])
        )
    for copy in copies:
        copy.start()
    for copy in copies:
        copy.wait()


def blocks_kernel(lanes, owners, *refs):
    held, (weight, across, keep, give, weight_out) = refs[:lanes], refs[lanes:]
    weight_out[...] = weight[...] + across[...]
    me = lax.axis_index("member")
    lane, plane = me % lanes, me // lanes

    def rows_of(block):
        place = (owners[block] % lanes) ^ lane
        rows = held[0][...]
        for k in range(1, lanes):
            rows = jnp.where(place == k, held[k][...], rows)
        return rows

    side = plane % 2
    for j in range(keep.shape[0]):
        keep[j] = rows_of(2 * j + side)
        give[j] = rows_of(2 * j + 1 - side)


def weight_rows(total, features):
    high = total.astype(BF16).astype(F32)
    middle = (total - high).astype(BF16).astype(F32)
    low = total - high - middle
    row = lax.broadcasted_iota(jnp.int32, (TAIL, features), 0)
    picked = jnp.where(row == 0, high, jnp.where(row == 1, middle, jnp.where(row == 2, low, 0.0)))
    return picked.astype(BF16)


def weight_from(rows):
    return jnp.sum(rows[:, 0:128].astype(F32), axis=0, keepdims=True)


def merged(lanes, owners, plane, bit, keep, got, j):
    block = j * (2 * bit) + plane % (2 * bit)
    there = ((owners[block] // lanes) ^ plane) // bit % 2
    return jnp.where(there == 1, got[j], keep[j])


def halve_kernel(lanes, bit, owners, keep, got, *refs):
    *weights, keep_out, give, weight_out = refs
    own, features = keep.shape[1], keep.shape[2]
    total = jnp.sum(sum((ref[...] for ref in weights[1:]), weights[0][...]), keepdims=True)
    weight_out[...] = jnp.broadcast_to(total, weight_out.shape)
    plane = lax.axis_index("member") // lanes
    side = plane // (2 * bit) % 2
    rows = [merged(lanes, owners, plane, bit, keep, got, j) for j in range(keep.shape[0])]
    for j in range(keep_out.shape[0]):
        keep_out[j] = jnp.where(side == 1, rows[2 * j + 1], rows[2 * j])
        give[pl.ds(j * own, own), :] = jnp.where(side == 1, rows[2 * j], rows[2 * j + 1])
    give[pl.ds(keep_out.shape[0] * own, TAIL), :] = weight_rows(total, features)


def fetch_kernel(inlet, outlet, after, inlet_near, outlet_near, sems):
    rows = pl.ds(0, outlet_near.shape[0])
    copies = [
        pltpu.make_async_copy(inlet, inlet_near, sems.at[0]),
        pltpu.make_async_copy(outlet.at[rows, :], outlet_near, sems.at[1]),
    ]
    for copy in copies:
        copy.start()
    for copy in copies:
        copy.wait()


def prepared(analyses, owners, area_weight, inlet, outlet, after):
    members, regions = lax.axis_size("member"), lax.axis_size("region")
    _, rows, features = analyses.shape
    blocks = owners.shape[0]
    lanes, own = members // blocks, rows // members
    row = jax.ShapeDtypeStruct((own, features), BF16)
    line = jax.ShapeDtypeStruct((1, own), F32)

    def kept(many):
        return jax.ShapeDtypeStruct((many, own, features), BF16)

    *by_lane, own_weight = local_call(
        functools.partial(rows_kernel, lanes),
        [row] * lanes + [line],
        [SMEM] + [HBM] * 2,
        scratch=[pltpu.SemaphoreType.DMA((lanes + 1,))],
        limit=ROWS_LIMIT,
    )(owners, analyses, area_weight[None])
    by_lane = [by_lane[0]] + [swap(by_lane[k], "member", k) for k in range(1, lanes)]
    weight = own_weight
    for bit in bits_of(regions)[:-1]:
        weight = weight + swap(weight, "region", bit)
    across = swap(weight, "region", regions // 2)
    keep, give, weight = local_call(
        functools.partial(blocks_kernel, lanes),
        [kept(blocks // 2)] * 2 + [line],
        [SMEM] + [VMEM] * (lanes + 2),
        limit=8,
    )(owners, *by_lane, weight, across)
    weights = [weight] + [swap(weight, "member", k) for k in range(1, lanes)]
    got = swap(give, "member", lanes)
    small = jax.ShapeDtypeStruct((8, 128), F32)
    keep, give, total = local_call(
        functools.partial(halve_kernel, lanes, 1),
        [kept(1), jax.ShapeDtypeStruct((own + TAIL, features), BF16), small],
        [SMEM] + [VMEM] * (2 + len(weights)),
        limit=8,
    )(owners, keep, got, *weights)
    got = swap(give, "member", 2 * lanes)
    near = local_call(
        fetch_kernel,
        [
            jax.ShapeDtypeStruct(inlet.shape, BF16),
            jax.ShapeDtypeStruct((outlet.shape[0] // HIDDEN_PIECES, features), BF16),
        ],
        [HBM, HBM, VMEM],
        moved=3 * inlet.size,
        scratch=[pltpu.SemaphoreType.DMA((2,))],
        limit=FETCH_LIMIT,
    )(inlet, outlet, after)
    got, *near = lax.optimization_barrier((got, *near))
    return keep, got, own_weight, total, *near


def column(row):
    size = row.shape[1]
    first = lax.broadcasted_iota(jnp.int32, (size, size), 0)
    second = lax.broadcasted_iota(jnp.int32, (size, size), 1)
    return jnp.sum(jnp.where(first == second, row, 0.0), axis=1, keepdims=True)


def network(noise, latent, hidden_piece, pieces):
    members, tokens, features = noise.shape
    states = (noise.astype(F32) + latent.astype(F32)[None]).reshape(members * tokens, features)
    mean = jnp.sum(states * states, axis=-1, keepdims=True) * (1.0 / features)
    normed = (states * lax.rsqrt(mean + EPSILON)).astype(BF16)
    total = states
    for piece in range(pieces):
        total = total + hidden_piece(normed, piece)
    return total.astype(BF16)


def score(forecast, targets, scale, members, tokens):
    rows, features = forecast.shape
    gram = lax.dot_general(
        forecast, forecast, (((1,), (1,)), ((), ())), preferred_element_type=F32
    )
    first = lax.broadcasted_iota(jnp.int32, (rows, rows), 0)
    second = lax.broadcasted_iota(jnp.int32, (rows, rows), 1)
    same_row = first == second
    same_token = (first % tokens) == (second % tokens)
    on_diagonal = jnp.where(same_row, gram, 0.0)
    down = jnp.sum(on_diagonal, axis=1, keepdims=True)
    across = jnp.sum(on_diagonal, axis=0, keepdims=True)
    squared = jnp.maximum((down + across - 2.0 * gram) * (1.0 / features), 0.0) + EPSILON
    inverse = lax.rsqrt(squared)
    pairs = jnp.where(same_token, squared * inverse, 0.0)
    coeff = jnp.where(same_token & ~same_row, inverse, 0.0).astype(BF16)
    coeff_sum = jnp.sum(coeff.astype(F32), axis=1, keepdims=True)
    combined = jnp.dot(coeff, forecast, preferred_element_type=F32)
    values = forecast.astype(F32)
    apart = (
        values.reshape(members, tokens, features) - targets.astype(F32)[None]
    )
    squares = jnp.sum(apart * apart, axis=-1, keepdims=True) * (1.0 / features) + EPSILON
    inverse_spread = lax.rsqrt(squares)
    from_others = (coeff_sum * values - combined).reshape(members, tokens, features)
    gradient = scale[None] * (apart * inverse_spread - from_others * (1.0 / members))
    spread = jnp.sum(squares * inverse_spread, axis=0) * (1.0 / members)
    pair_sum = jnp.sum(jnp.sum(pairs, axis=1, keepdims=True).reshape(members, tokens, 1), axis=0)
    energy = scale * (spread - pair_sum * (1.0 / (2.0 * members * members)))
    return gradient, energy


def member_kernel(
    lanes,
    bit,
    owners,
    keep,
    got,
    encoder,
    weight,
    total,
    noise,
    inlet,
    outlet_near,
    targets_hbm,
    outlet_hbm,
    gradient_hbm,
    energy_out,
    total_out,
    targets,
    outlet,
    hidden,
    gradient_near,
    sems,
    out_sems,
):
    members, own, features = noise.shape
    width = inlet.shape[1] // HIDDEN_PIECES
    copies = [pltpu.make_async_copy(targets_hbm, targets, sems.at[0])]
    for piece in range(1, HIDDEN_PIECES):
        copies.append(
            pltpu.make_async_copy(
                outlet_hbm.at[pl.ds(piece * width, width), :],
                outlet.at[pl.ds((piece - 1) * width, width), :],
                sems.at[piece],
            )
        )
    for copy in copies:
        copy.start()

    def hidden_piece(normed, piece):
        columns = slice(piece * width, (piece + 1) * width)
        hidden[...] = jax.nn.gelu(
            jnp.dot(normed, inlet[:, columns], preferred_element_type=F32), approximate=True
        ).astype(BF16)
        if piece == 0:
            matrix = outlet_near[...]
        else:
            copies[piece].wait()
            matrix = outlet[(piece - 1) * width : piece * width, :]
        return jnp.dot(hidden[...], matrix, preferred_element_type=F32)

    plane = lax.axis_index("member") // lanes
    control = merged(lanes, owners, plane, bit, keep, [got[pl.ds(0, own), :]], 0)
    latent = jnp.dot(control, encoder[...], preferred_element_type=F32).astype(BF16)
    total_out[...] = total[...] + weight_from(got[pl.ds(own, TAIL), :])
    forecast = network(noise[...], latent, hidden_piece, HIDDEN_PIECES)
    forecast = forecast.reshape(members, own, features)
    copies[0].wait()
    scales = column(weight[...])
    returns = []
    for first in range(0, own, TOKENS_AT_ONCE):
        here = slice(first, first + TOKENS_AT_ONCE)
        gradient, energy = score(
            forecast[:, here].reshape(members * TOKENS_AT_ONCE, features),
            targets[here, :],
            scales[here, :],
            members,
            TOKENS_AT_ONCE,
        )
        gradient_near[:, here, :] = gradient.astype(BF16)
        energy_out[here, :] = energy
        tokens = pl.ds(first, TOKENS_AT_ONCE)
        returns.append(
            pltpu.make_async_copy(
                gradient_near.at[:, tokens, :],
                gradient_hbm.at[:, tokens, :],
                out_sems.at[len(returns)],
            )
        )
        returns[-1].start()
    for copy in returns:
        copy.wait()


def on_device(
    analyses,
    owners,
    noise,
    targets,
    area_weight,
    enc_weight,
    sample_inlet_matrix,
    sample_outlet_matrix,
):
    members, regions = lax.axis_size("member"), lax.axis_size("region")
    _, region_rows, features = noise.shape
    hidden = sample_inlet_matrix.shape[1]
    own = region_rows // members
    here = transposed(noise.reshape(members, own, features))
    keep, got, weight, total, inlet, outlet_near = prepared(
        analyses, owners, area_weight, sample_inlet_matrix, sample_outlet_matrix, here
    )
    lanes = members // owners.shape[0]
    gradient, energy, total = local_call(
        functools.partial(member_kernel, lanes, owners.shape[0] // 2),
        [
            jax.ShapeDtypeStruct((members, own, features), BF16),
            jax.ShapeDtypeStruct((own, 1), F32),
            jax.ShapeDtypeStruct((8, 128), F32),
        ],
        [SMEM] + [VMEM] * 8 + [HBM] * 2,
        flops=4 * members * own * features * (hidden + members),
        moved=4 * features * hidden,
        scratch=[
            pltpu.VMEM((own, features), BF16),
            pltpu.VMEM((hidden - hidden // HIDDEN_PIECES, features), BF16),
            pltpu.VMEM((members * own, hidden // HIDDEN_PIECES), BF16),
            pltpu.VMEM((members, own, features), BF16),
            pltpu.SemaphoreType.DMA((HIDDEN_PIECES,)),
            pltpu.SemaphoreType.DMA((own // TOKENS_AT_ONCE,)),
        ],
        limit=NETWORK_LIMIT,
        out_specs=[HBM, VMEM, VMEM],
    )(
        owners,
        keep,
        got,
        enc_weight,
        weight,
        total,
        here,
        inlet,
        outlet_near,
        targets,
        sample_outlet_matrix,
    )
    gradient, total = lax.optimization_barrier((gradient, total))
    back = transposed(gradient)
    across = swap(total, "member", lanes)
    factor = float(region_rows * regions) / (total[0, 0] + across[0, 0])
    member_grad = (back.astype(F32) * factor).astype(BF16).reshape(1, region_rows, features)
    return member_grad, energy[:, 0] * factor


def solution(mesh):
    return jax.shard_map(
        on_device,
        mesh=mesh,
        in_specs=(
            P("member", "region", None),
            P(),
            P("member", "region", None),
            P(("region", "member"), None),
            P(("region", "member")),
            P(),
            P(),
            P(),
        ),
        out_specs=(P("member", "region", None), P(("region", "member"))),
        check_vma=False,
    )
```

```python
import functools

import jax
import jax.numpy as jnp
from jax import lax
from jax.experimental import pallas as pl
from jax.experimental.pallas import tpu as pltpu
from jax.sharding import PartitionSpec as P

EPSILON = 1e-06
TOKENS_AT_ONCE = 16
TAIL = 16
ROWS_LIMIT = 53
NETWORK_LIMIT = 32
ENCODE_LIMIT = 46
FETCH_LIMIT = 44
BF16 = jnp.bfloat16
F32 = jnp.float32

VMEM = pl.BlockSpec(memory_space=pltpu.VMEM)
SMEM = pl.BlockSpec(memory_space=pltpu.SMEM)
HBM = pl.BlockSpec(memory_space=pltpu.HBM)


def swap(value, axis, bit):
    size = lax.axis_size(axis)
    return lax.ppermute(value, axis, [(i, i ^ bit) for i in range(size)])


def bits_of(size):
    return [1 << i for i in range(size.bit_length() - 1)]


def transposed(value):
    return lax.all_to_all(value, "member", split_axis=0, concat_axis=0, tiled=True)


def local_call(kernel, out_shape, in_specs, flops=0, moved=0, scratch=(), limit=40):
    return pl.pallas_call(
        kernel,
        in_specs=in_specs,
        out_specs=[VMEM] * len(out_shape),
        out_shape=out_shape,
        scratch_shapes=list(scratch),
        compiler_params=pltpu.CompilerParams(vmem_limit_bytes=limit * 2**20),
        cost_estimate=pl.CostEstimate(flops=flops, bytes_accessed=moved, transcendentals=0),
    )


def rows_kernel(lanes, owners, analyses, weight, *refs):
    *outs, weight_out, sems = refs
    own = outs[0].shape[0]
    me = lax.axis_index("member")
    lane = me % lanes
    block = jnp.int32(0)
    for b in range(owners.shape[0]):
        block = jnp.where(owners[b] == me, b, block)
    copies = [
        pltpu.make_async_copy(weight, weight_out, sems.at[lanes]),
    ]
    for k in range(lanes):
        start = pl.multiple_of((block * lanes + (lane ^ k)) * own, own)
        copies.append(
            pltpu.make_async_copy(analyses.at[0, pl.ds(start, own), :], outs[k], sems.at[k])
        )
    for copy in copies:
        copy.start()
    for copy in copies:
        copy.wait()


def blocks_kernel(lanes, owners, *refs):
    held, (weight, across, keep, give, weight_out) = refs[:lanes], refs[lanes:]
    weight_out[...] = weight[...] + across[...]
    me = lax.axis_index("member")
    lane, plane = me % lanes, me // lanes

    def rows_of(block):
        place = (owners[block] % lanes) ^ lane
        rows = held[0][...]
        for k in range(1, lanes):
            rows = jnp.where(place == k, held[k][...], rows)
        return rows

    side = plane % 2
    for j in range(keep.shape[0]):
        keep[j] = rows_of(2 * j + side)
        give[j] = rows_of(2 * j + 1 - side)


def weight_rows(total, features):
    high = total.astype(BF16).astype(F32)
    middle = (total - high).astype(BF16).astype(F32)
    low = total - high - middle
    row = lax.broadcasted_iota(jnp.int32, (TAIL, features), 0)
    picked = jnp.where(row == 0, high, jnp.where(row == 1, middle, jnp.where(row == 2, low, 0.0)))
    return picked.astype(BF16)


def weight_from(rows):
    return jnp.sum(rows[:, 0:128].astype(F32), axis=0, keepdims=True)


def merged(lanes, owners, plane, bit, keep, got, j):
    block = j * (2 * bit) + plane % (2 * bit)
    there = ((owners[block] // lanes) ^ plane) // bit % 2
    return jnp.where(there == 1, got[j], keep[j])


def halve_kernel(lanes, bit, owners, keep, got, *refs):
    *weights, keep_out, give, weight_out = refs
    own, features = keep.shape[1], keep.shape[2]
    total = jnp.sum(sum((ref[...] for ref in weights[1:]), weights[0][...]), keepdims=True)
    weight_out[...] = jnp.broadcast_to(total, weight_out.shape)
    plane = lax.axis_index("member") // lanes
    side = plane // (2 * bit) % 2
    rows = [merged(lanes, owners, plane, bit, keep, got, j) for j in range(keep.shape[0])]
    for j in range(keep_out.shape[0]):
        keep_out[j] = jnp.where(side == 1, rows[2 * j + 1], rows[2 * j])
        give[pl.ds(j * own, own), :] = jnp.where(side == 1, rows[2 * j], rows[2 * j + 1])
    give[pl.ds(keep_out.shape[0] * own, TAIL), :] = weight_rows(total, features)


def fetch_kernel(inlet, outlet, after, inlet_near, outlet_near, sems):
    rows = pl.ds(0, outlet_near.shape[0])
    copies = [
        pltpu.make_async_copy(inlet, inlet_near, sems.at[0]),
        pltpu.make_async_copy(outlet.at[rows, :], outlet_near, sems.at[1]),
    ]
    for copy in copies:
        copy.start()
    for copy in copies:
        copy.wait()


def encode_kernel(
    lanes, bit, owners, keep, got, encoder, total, outlet, latent, total_out, outlet_near, sem
):
    half = outlet_near.shape[0]
    copy = pltpu.make_async_copy(outlet.at[pl.ds(half, half), :], outlet_near, sem)
    copy.start()
    own = latent.shape[0]
    plane = lax.axis_index("member") // lanes
    rows = [got[pl.ds(0, own), :]]
    control = merged(lanes, owners, plane, bit, keep, rows, 0)
    latent[...] = jnp.dot(control, encoder[...], preferred_element_type=F32).astype(BF16)
    total_out[...] = total[...] + weight_from(got[pl.ds(own, TAIL), :])
    copy.wait()


def prepared(analyses, owners, encoder, area_weight, inlet, outlet, after):
    members, regions = lax.axis_size("member"), lax.axis_size("region")
    _, rows, features = analyses.shape
    blocks = owners.shape[0]
    lanes, own = members // blocks, rows // members
    row = jax.ShapeDtypeStruct((own, features), BF16)
    line = jax.ShapeDtypeStruct((1, own), F32)

    def kept(many):
        return jax.ShapeDtypeStruct((many, own, features), BF16)

    *by_lane, own_weight = local_call(
        functools.partial(rows_kernel, lanes),
        [row] * lanes + [line],
        [SMEM] + [HBM] * 2,
        scratch=[pltpu.SemaphoreType.DMA((lanes + 1,))],
        limit=ROWS_LIMIT,
    )(owners, analyses, area_weight[None])
    by_lane = [by_lane[0]] + [swap(by_lane[k], "member", k) for k in range(1, lanes)]
    weight = own_weight
    for bit in bits_of(regions)[:-1]:
        weight = weight + swap(weight, "region", bit)
    across = swap(weight, "region", regions // 2)
    keep, give, weight = local_call(
        functools.partial(blocks_kernel, lanes),
        [kept(blocks // 2)] * 2 + [line],
        [SMEM] + [VMEM] * (lanes + 2),
        limit=8,
    )(owners, *by_lane, weight, across)
    weights = [weight] + [swap(weight, "member", k) for k in range(1, lanes)]
    got = swap(give, "member", lanes)
    small = jax.ShapeDtypeStruct((8, 128), F32)
    keep, give, total = local_call(
        functools.partial(halve_kernel, lanes, 1),
        [kept(1), jax.ShapeDtypeStruct((own + TAIL, features), BF16), small],
        [SMEM] + [VMEM] * (2 + len(weights)),
        limit=8,
    )(owners, keep, got, *weights)
    got = swap(give, "member", 2 * lanes)
    half = jax.ShapeDtypeStruct((outlet.shape[0] // 2, features), BF16)
    inlet, first_half = local_call(
        fetch_kernel,
        [jax.ShapeDtypeStruct(inlet.shape, BF16), half],
        [HBM, HBM, VMEM],
        moved=3 * inlet.size,
        scratch=[pltpu.SemaphoreType.DMA((2,))],
        limit=FETCH_LIMIT,
    )(inlet, outlet, after)
    got, inlet, first_half = lax.optimization_barrier((got, inlet, first_half))
    latent, total, second_half = local_call(
        functools.partial(encode_kernel, lanes, 2),
        [row, small, half],
        [SMEM] + [VMEM] * 4 + [HBM],
        flops=2 * own * features * features,
        scratch=[pltpu.SemaphoreType.DMA],
        limit=ENCODE_LIMIT,
    )(owners, keep, got, encoder, total, outlet)
    return latent, own_weight, total, inlet, first_half, second_half


def column(row):
    size = row.shape[1]
    first = lax.broadcasted_iota(jnp.int32, (size, size), 0)
    second = lax.broadcasted_iota(jnp.int32, (size, size), 1)
    return jnp.sum(jnp.where(first == second, row, 0.0), axis=1, keepdims=True)


def network(noise, latent, hidden_piece, pieces):
    members, tokens, features = noise.shape
    states = (noise.astype(F32) + latent.astype(F32)[None]).reshape(members * tokens, features)
    mean = jnp.sum(states * states, axis=-1, keepdims=True) * (1.0 / features)
    normed = (states * lax.rsqrt(mean + EPSILON)).astype(BF16)
    total = states
    for piece in range(pieces):
        total = total + hidden_piece(normed, piece)
    return total.astype(BF16)


def score(forecast, targets, scale, members, tokens):
    rows, features = forecast.shape
    gram = lax.dot_general(
        forecast, forecast, (((1,), (1,)), ((), ())), preferred_element_type=F32
    )
    first = lax.broadcasted_iota(jnp.int32, (rows, rows), 0)
    second = lax.broadcasted_iota(jnp.int32, (rows, rows), 1)
    same_row = first == second
    same_token = (first % tokens) == (second % tokens)
    on_diagonal = jnp.where(same_row, gram, 0.0)
    down = jnp.sum(on_diagonal, axis=1, keepdims=True)
    across = jnp.sum(on_diagonal, axis=0, keepdims=True)
    squared = jnp.maximum((down + across - 2.0 * gram) * (1.0 / features), 0.0) + EPSILON
    inverse = lax.rsqrt(squared)
    pairs = jnp.where(same_token, squared * inverse, 0.0)
    coeff = jnp.where(same_token & ~same_row, inverse, 0.0).astype(BF16)
    coeff_sum = jnp.sum(coeff.astype(F32), axis=1, keepdims=True)
    combined = jnp.dot(coeff, forecast, preferred_element_type=F32)
    values = forecast.astype(F32)
    apart = (
        values.reshape(members, tokens, features) - targets.astype(F32)[None]
    )
    squares = jnp.sum(apart * apart, axis=-1, keepdims=True) * (1.0 / features) + EPSILON
    inverse_spread = lax.rsqrt(squares)
    from_others = (coeff_sum * values - combined).reshape(members, tokens, features)
    gradient = scale[None] * (apart * inverse_spread - from_others * (1.0 / members))
    spread = jnp.sum(squares * inverse_spread, axis=0) * (1.0 / members)
    pair_sum = jnp.sum(jnp.sum(pairs, axis=1, keepdims=True).reshape(members, tokens, 1), axis=0)
    energy = scale * (spread - pair_sum * (1.0 / (2.0 * members * members)))
    return gradient, energy


def member_kernel(
    noise,
    latent,
    weight,
    inlet,
    first_half,
    second_half,
    targets_hbm,
    gradient_out,
    energy_out,
    targets,
    hidden,
    sem,
):
    members, own, features = noise.shape
    aside = pltpu.make_async_copy(targets_hbm, targets, sem)
    aside.start()
    halves = (first_half, second_half)
    width = first_half.shape[0]

    def hidden_piece(normed, piece):
        columns = slice(piece * width, (piece + 1) * width)
        hidden[...] = jax.nn.gelu(
            jnp.dot(normed, inlet[:, columns], preferred_element_type=F32), approximate=True
        ).astype(BF16)
        return jnp.dot(hidden[...], halves[piece][...], preferred_element_type=F32)

    forecast = network(noise[...], latent[...], hidden_piece, len(halves))
    forecast = forecast.reshape(members, own, features)
    aside.wait()
    scales = column(weight[...])
    for first in range(0, own, TOKENS_AT_ONCE):
        here = slice(first, first + TOKENS_AT_ONCE)
        gradient, energy = score(
            forecast[:, here].reshape(members * TOKENS_AT_ONCE, features),
            targets[here, :],
            scales[here, :],
            members,
            TOKENS_AT_ONCE,
        )
        gradient_out[:, here, :] = gradient.astype(BF16)
        energy_out[here, :] = energy


def on_device(
    analyses,
    owners,
    noise,
    targets,
    area_weight,
    enc_weight,
    sample_inlet_matrix,
    sample_outlet_matrix,
):
    members, regions = lax.axis_size("member"), lax.axis_size("region")
    _, region_rows, features = noise.shape
    hidden = sample_inlet_matrix.shape[1]
    own = region_rows // members
    here = transposed(noise.reshape(members, own, features))
    latent, weight, total, *matrices = prepared(
        analyses,
        owners,
        enc_weight,
        area_weight,
        sample_inlet_matrix,
        sample_outlet_matrix,
        here,
    )
    gradient, energy = local_call(
        member_kernel,
        [
            jax.ShapeDtypeStruct((members, own, features), BF16),
            jax.ShapeDtypeStruct((own, 1), F32),
        ],
        [VMEM] * 6 + [HBM],
        flops=4 * members * own * features * (hidden + members),
        moved=4 * features * hidden,
        scratch=[
            pltpu.VMEM((own, features), BF16),
            pltpu.VMEM((members * own, hidden // 2), BF16),
            pltpu.SemaphoreType.DMA,
        ],
        limit=NETWORK_LIMIT,
    )(here, latent, weight, *matrices, targets)
    gradient, total = lax.optimization_barrier((gradient, total))
    back = transposed(gradient)
    across = swap(total, "member", members // owners.shape[0])
    factor = float(region_rows * regions) / (total[0, 0] + across[0, 0])
    member_grad = (back.astype(F32) * factor).astype(BF16).reshape(1, region_rows, features)
    return member_grad, energy[:, 0] * factor


def solution(mesh):
    return jax.shard_map(
        on_device,
        mesh=mesh,
        in_specs=(
            P("member", "region", None),
            P(),
            P("member", "region", None),
            P(("region", "member"), None),
            P(("region", "member")),
            P(),
            P(),
            P(),
        ),
        out_specs=(P("member", "region", None), P(("region", "member"))),
        check_vma=False,
    )
```

```python
import functools

import jax
import jax.numpy as jnp
from jax import lax
from jax.experimental import pallas as pl
from jax.experimental.pallas import tpu as pltpu
from jax.sharding import PartitionSpec as P

EPSILON = 1e-06
TOKENS_AT_ONCE = 16
TAIL = 16
ROWS_LIMIT = 53
NETWORK_LIMIT = 44
FETCH_LIMIT = 44
BF16 = jnp.bfloat16
F32 = jnp.float32

VMEM = pl.BlockSpec(memory_space=pltpu.VMEM)
SMEM = pl.BlockSpec(memory_space=pltpu.SMEM)
HBM = pl.BlockSpec(memory_space=pltpu.HBM)


def swap(value, axis, bit):
    size = lax.axis_size(axis)
    return lax.ppermute(value, axis, [(i, i ^ bit) for i in range(size)])


def bits_of(size):
    return [1 << i for i in range(size.bit_length() - 1)]


def transposed(value):
    return lax.all_to_all(value, "member", split_axis=0, concat_axis=0, tiled=True)


def local_call(kernel, out_shape, in_specs, flops=0, moved=0, scratch=(), limit=40):
    return pl.pallas_call(
        kernel,
        in_specs=in_specs,
        out_specs=[VMEM] * len(out_shape),
        out_shape=out_shape,
        scratch_shapes=list(scratch),
        compiler_params=pltpu.CompilerParams(vmem_limit_bytes=limit * 2**20),
        cost_estimate=pl.CostEstimate(flops=flops, bytes_accessed=moved, transcendentals=0),
    )


def rows_kernel(lanes, owners, analyses, weight, *refs):
    *outs, weight_out, sems = refs
    own = outs[0].shape[0]
    me = lax.axis_index("member")
    lane = me % lanes
    block = jnp.int32(0)
    for b in range(owners.shape[0]):
        block = jnp.where(owners[b] == me, b, block)
    copies = [
        pltpu.make_async_copy(weight, weight_out, sems.at[lanes]),
    ]
    for k in range(lanes):
        start = pl.multiple_of((block * lanes + (lane ^ k)) * own, own)
        copies.append(
            pltpu.make_async_copy(analyses.at[0, pl.ds(start, own), :], outs[k], sems.at[k])
        )
    for copy in copies:
        copy.start()
    for copy in copies:
        copy.wait()


def blocks_kernel(lanes, owners, *refs):
    held, (weight, across, keep, give, weight_out) = refs[:lanes], refs[lanes:]
    weight_out[...] = weight[...] + across[...]
    me = lax.axis_index("member")
    lane, plane = me % lanes, me // lanes

    def rows_of(block):
        place = (owners[block] % lanes) ^ lane
        rows = held[0][...]
        for k in range(1, lanes):
            rows = jnp.where(place == k, held[k][...], rows)
        return rows

    side = plane % 2
    for j in range(keep.shape[0]):
        keep[j] = rows_of(2 * j + side)
        give[j] = rows_of(2 * j + 1 - side)


def weight_rows(total, features):
    high = total.astype(BF16).astype(F32)
    middle = (total - high).astype(BF16).astype(F32)
    low = total - high - middle
    row = lax.broadcasted_iota(jnp.int32, (TAIL, features), 0)
    picked = jnp.where(row == 0, high, jnp.where(row == 1, middle, jnp.where(row == 2, low, 0.0)))
    return picked.astype(BF16)


def weight_from(rows):
    return jnp.sum(rows[:, 0:128].astype(F32), axis=0, keepdims=True)


def merged(lanes, owners, plane, bit, keep, got, j):
    block = j * (2 * bit) + plane % (2 * bit)
    there = ((owners[block] // lanes) ^ plane) // bit % 2
    return jnp.where(there == 1, got[j], keep[j])


def halve_kernel(lanes, bit, owners, keep, got, *refs):
    *weights, keep_out, give, weight_out = refs
    own, features = keep.shape[1], keep.shape[2]
    total = jnp.sum(sum((ref[...] for ref in weights[1:]), weights[0][...]), keepdims=True)
    weight_out[...] = jnp.broadcast_to(total, weight_out.shape)
    plane = lax.axis_index("member") // lanes
    side = plane // (2 * bit) % 2
    rows = [merged(lanes, owners, plane, bit, keep, got, j) for j in range(keep.shape[0])]
    for j in range(keep_out.shape[0]):
        keep_out[j] = jnp.where(side == 1, rows[2 * j + 1], rows[2 * j])
        give[pl.ds(j * own, own), :] = jnp.where(side == 1, rows[2 * j], rows[2 * j + 1])
    give[pl.ds(keep_out.shape[0] * own, TAIL), :] = weight_rows(total, features)


def fetch_kernel(inlet, outlet, after, inlet_near, outlet_near, sems):
    rows = pl.ds(0, outlet_near.shape[0])
    copies = [
        pltpu.make_async_copy(inlet, inlet_near, sems.at[0]),
        pltpu.make_async_copy(outlet.at[rows, :], outlet_near, sems.at[1]),
    ]
    for copy in copies:
        copy.start()
    for copy in copies:
        copy.wait()


def encode_kernel(lanes, bit, owners, keep, got, encoder, total, latent, total_out):
    own = latent.shape[0]
    plane = lax.axis_index("member") // lanes
    rows = [got[pl.ds(0, own), :]]
    control = merged(lanes, owners, plane, bit, keep, rows, 0)
    latent[...] = jnp.dot(control, encoder[...], preferred_element_type=F32).astype(BF16)
    total_out[...] = total[...] + weight_from(got[pl.ds(own, TAIL), :])


def prepared(analyses, owners, encoder, area_weight, inlet, outlet, after):
    members, regions = lax.axis_size("member"), lax.axis_size("region")
    _, rows, features = analyses.shape
    blocks = owners.shape[0]
    lanes, own = members // blocks, rows // members
    row = jax.ShapeDtypeStruct((own, features), BF16)
    line = jax.ShapeDtypeStruct((1, own), F32)

    def kept(many):
        return jax.ShapeDtypeStruct((many, own, features), BF16)

    *by_lane, own_weight = local_call(
        functools.partial(rows_kernel, lanes),
        [row] * lanes + [line],
        [SMEM] + [HBM] * 2,
        scratch=[pltpu.SemaphoreType.DMA((lanes + 1,))],
        limit=ROWS_LIMIT,
    )(owners, analyses, area_weight[None])
    by_lane = [by_lane[0]] + [swap(by_lane[k], "member", k) for k in range(1, lanes)]
    weight = own_weight
    for bit in bits_of(regions)[:-1]:
        weight = weight + swap(weight, "region", bit)
    across = swap(weight, "region", regions // 2)
    keep, give, weight = local_call(
        functools.partial(blocks_kernel, lanes),
        [kept(blocks // 2)] * 2 + [line],
        [SMEM] + [VMEM] * (lanes + 2),
        limit=8,
    )(owners, *by_lane, weight, across)
    weights = [weight] + [swap(weight, "member", k) for k in range(1, lanes)]
    got = swap(give, "member", lanes)
    small = jax.ShapeDtypeStruct((8, 128), F32)
    keep, give, total = local_call(
        functools.partial(halve_kernel, lanes, 1),
        [kept(1), jax.ShapeDtypeStruct((own + TAIL, features), BF16), small],
        [SMEM] + [VMEM] * (2 + len(weights)),
        limit=8,
    )(owners, keep, got, *weights)
    got = swap(give, "member", 2 * lanes)
    half = jax.ShapeDtypeStruct((outlet.shape[0] // 2, features), BF16)
    inlet, first_half = local_call(
        fetch_kernel,
        [jax.ShapeDtypeStruct(inlet.shape, BF16), half],
        [HBM, HBM, VMEM],
        moved=3 * inlet.size,
        scratch=[pltpu.SemaphoreType.DMA((2,))],
        limit=FETCH_LIMIT,
    )(inlet, outlet, after)
    got, inlet, first_half = lax.optimization_barrier((got, inlet, first_half))
    latent, total = local_call(
        functools.partial(encode_kernel, lanes, 2),
        [row, small],
        [SMEM] + [VMEM] * 4,
        flops=2 * own * features * features,
        limit=8,
    )(owners, keep, got, encoder, total)
    return latent, own_weight, total, inlet, first_half


def column(row):
    size = row.shape[1]
    first = lax.broadcasted_iota(jnp.int32, (size, size), 0)
    second = lax.broadcasted_iota(jnp.int32, (size, size), 1)
    return jnp.sum(jnp.where(first == second, row, 0.0), axis=1, keepdims=True)


def network(noise, latent, hidden_piece, pieces):
    members, tokens, features = noise.shape
    states = (noise.astype(F32) + latent.astype(F32)[None]).reshape(members * tokens, features)
    mean = jnp.sum(states * states, axis=-1, keepdims=True) * (1.0 / features)
    normed = (states * lax.rsqrt(mean + EPSILON)).astype(BF16)
    total = states
    for piece in range(pieces):
        total = total + hidden_piece(normed, piece)
    return total.astype(BF16)


def score(forecast, targets, scale, members, tokens):
    rows, features = forecast.shape
    gram = lax.dot_general(
        forecast, forecast, (((1,), (1,)), ((), ())), preferred_element_type=F32
    )
    first = lax.broadcasted_iota(jnp.int32, (rows, rows), 0)
    second = lax.broadcasted_iota(jnp.int32, (rows, rows), 1)
    same_row = first == second
    same_token = (first % tokens) == (second % tokens)
    on_diagonal = jnp.where(same_row, gram, 0.0)
    down = jnp.sum(on_diagonal, axis=1, keepdims=True)
    across = jnp.sum(on_diagonal, axis=0, keepdims=True)
    squared = jnp.maximum((down + across - 2.0 * gram) * (1.0 / features), 0.0) + EPSILON
    inverse = lax.rsqrt(squared)
    pairs = jnp.where(same_token, squared * inverse, 0.0)
    coeff = jnp.where(same_token & ~same_row, inverse, 0.0).astype(BF16)
    coeff_sum = jnp.sum(coeff.astype(F32), axis=1, keepdims=True)
    combined = jnp.dot(coeff, forecast, preferred_element_type=F32)
    values = forecast.astype(F32)
    apart = (
        values.reshape(members, tokens, features) - targets.astype(F32)[None]
    )
    squares = jnp.sum(apart * apart, axis=-1, keepdims=True) * (1.0 / features) + EPSILON
    inverse_spread = lax.rsqrt(squares)
    from_others = (coeff_sum * values - combined).reshape(members, tokens, features)
    gradient = scale[None] * (apart * inverse_spread - from_others * (1.0 / members))
    spread = jnp.sum(squares * inverse_spread, axis=0) * (1.0 / members)
    pair_sum = jnp.sum(jnp.sum(pairs, axis=1, keepdims=True).reshape(members, tokens, 1), axis=0)
    energy = scale * (spread - pair_sum * (1.0 / (2.0 * members * members)))
    return gradient, energy


def member_kernel(
    noise,
    latent,
    weight,
    inlet,
    first_half,
    targets_hbm,
    outlet_hbm,
    gradient_out,
    energy_out,
    targets,
    second_half,
    hidden,
    sems,
):
    members, own, features = noise.shape
    width = first_half.shape[0]
    rest = pltpu.make_async_copy(outlet_hbm.at[pl.ds(width, width), :], second_half, sems.at[0])
    aside = pltpu.make_async_copy(targets_hbm, targets, sems.at[1])
    rest.start()
    aside.start()
    halves = (first_half, second_half)

    def hidden_piece(normed, piece):
        columns = slice(piece * width, (piece + 1) * width)
        hidden[...] = jax.nn.gelu(
            jnp.dot(normed, inlet[:, columns], preferred_element_type=F32), approximate=True
        ).astype(BF16)
        if piece == 1:
            rest.wait()
        return jnp.dot(hidden[...], halves[piece][...], preferred_element_type=F32)

    forecast = network(noise[...], latent[...], hidden_piece, len(halves))
    forecast = forecast.reshape(members, own, features)
    aside.wait()
    scales = column(weight[...])
    for first in range(0, own, TOKENS_AT_ONCE):
        here = slice(first, first + TOKENS_AT_ONCE)
        gradient, energy = score(
            forecast[:, here].reshape(members * TOKENS_AT_ONCE, features),
            targets[here, :],
            scales[here, :],
            members,
            TOKENS_AT_ONCE,
        )
        gradient_out[:, here, :] = gradient.astype(BF16)
        energy_out[here, :] = energy


def on_device(
    analyses,
    owners,
    noise,
    targets,
    area_weight,
    enc_weight,
    sample_inlet_matrix,
    sample_outlet_matrix,
):
    members, regions = lax.axis_size("member"), lax.axis_size("region")
    _, region_rows, features = noise.shape
    hidden = sample_inlet_matrix.shape[1]
    own = region_rows // members
    here = transposed(noise.reshape(members, own, features))
    latent, weight, total, *matrices = prepared(
        analyses,
        owners,
        enc_weight,
        area_weight,
        sample_inlet_matrix,
        sample_outlet_matrix,
        here,
    )
    gradient, energy = local_call(
        member_kernel,
        [
            jax.ShapeDtypeStruct((members, own, features), BF16),
            jax.ShapeDtypeStruct((own, 1), F32),
        ],
        [VMEM] * 5 + [HBM] * 2,
        flops=4 * members * own * features * (hidden + members),
        moved=4 * features * hidden,
        scratch=[
            pltpu.VMEM((own, features), BF16),
            pltpu.VMEM((hidden // 2, features), BF16),
            pltpu.VMEM((members * own, hidden // 2), BF16),
            pltpu.SemaphoreType.DMA((2,)),
        ],
        limit=NETWORK_LIMIT,
    )(here, latent, weight, *matrices, targets, sample_outlet_matrix)
    gradient, total = lax.optimization_barrier((gradient, total))
    back = transposed(gradient)
    across = swap(total, "member", members // owners.shape[0])
    factor = float(region_rows * regions) / (total[0, 0] + across[0, 0])
    member_grad = (back.astype(F32) * factor).astype(BF16).reshape(1, region_rows, features)
    return member_grad, energy[:, 0] * factor


def solution(mesh):
    return jax.shard_map(
        on_device,
        mesh=mesh,
        in_specs=(
            P("member", "region", None),
            P(),
            P("member", "region", None),
            P(("region", "member"), None),
            P(("region", "member")),
            P(),
            P(),
            P(),
        ),
        out_specs=(P("member", "region", None), P(("region", "member"))),
        check_vma=False,
    )
```
